32 devices in a mesh: rep: 16 (over z, y, core), shard: 2 (over x).
Axes of the slice: x: 2, y: 2, z: 4, core: 2. Of those that a mesh axis runs over, the one named last changes fastest.
Arguments:
- tokens: bfloat16 [32768, 576], P(('rep', 'shard')), may hold values from -6 to 6
- cotangent: bfloat16 [32768, 576], P(('rep', 'shard')), may hold values from -6 to 6
- lengths: int32 [32, 4], P(('rep', 'shard')), may hold values from 1 to 512, 1024 in all within a row
- w_query: bfloat16 [576, 576], P('shard'), may hold values from -0.25 to 0.25
- w_key: bfloat16 [576, 192], P('shard'), may hold values from -0.25 to 0.25
- w_value: bfloat16 [576, 192], P('shard'), may hold values from -0.25 to 0.25
- w_out: bfloat16 [576, 576], P('shard'), may hold values from -1 to 1
- attn_gain: bfloat16 [576], P('shard'), may hold values from 0.099609375 to 1.8984375
- w_gate: bfloat16 [576, 1536], P('shard'), may hold values from -0.25 to 0.25
- w_up: bfloat16 [576, 1536], P('shard'), may hold values from -0.25 to 0.25
- w_down: bfloat16 [1536, 576], P('shard'), may hold values from -0.21875 to 0.21875
- mlp_gain: bfloat16 [576], P('shard'), may hold values from 0.099609375 to 1.8984375
Outputs:
- output: bfloat16 [32768, 576], P(('rep', 'shard'))
- d_tokens: float32 [32768, 576], P(('rep', 'shard'))
- grad_query: float32 [576, 576], P('shard')
- grad_key: float32 [576, 192], P('shard')
- grad_value: float32 [576, 192], P('shard')
- grad_out: float32 [576, 576], P('shard')
- grad_attn_gain: float32 [576], P('shard')
- grad_gate: float32 [576, 1536], P('shard')
- grad_up: float32 [576, 1536], P('shard')
- grad_down: float32 [1536, 576], P('shard')
- grad_mlp_gain: float32 [576], P('shard')
The draws below stay inside these ranges and needn't reach their ends.
Inputs may be any that keep to these rules, and one draw needn't show every extreme that they name: Each row of lengths sums to 1024, and one entry of every row is exactly 512.
All inputs are finite; a program needn't handle non-finite values.
Results may differ from the reference program's by a relative error of at most 0.015.
Values may be sent and summed in bfloat16 or wider, within the bound.
No kernel may reach another device: no remote copies, remote signals or barrier semaphores. Data moves between devices by JAX's collectives and lax.ppermute only.
A program may use at most 192 MiB of HBM per device.

```python
import math
import jax
import jax.numpy as jnp
import numpy as np
from jax import lax

D = 576
H = 9
KVH = 3
HD = 64
FF = 1536
TOK_DEV = 1024
MAXLEN = 512
NDOC = 4
KV = 192
TOKENS = 32768
DEVICES = 32


def steps_of(stream_key, extent, cuts, smallest, top_value):
    level, own = 1.0, jax.random.fold_in(stream_key, 6)
    for axis_at, parts in cuts:
        draws = jnp.exp(jax.random.uniform(jax.random.fold_in(own, axis_at), (parts,), jnp.float32, smallest / len(cuts), top_value / len(cuts)))
        level = level * jnp.repeat(draws, extent[axis_at] // parts).reshape([-1 if axis == axis_at else 1 for axis in range(len(extent))])
    return level


def length_profile(number_of, total, bound, slope):
    weights = [(1 << 20) // math.isqrt(grade ** slope) + 1 for grade in range(2, number_of + 1)]
    spare, counts = total - bound - (number_of - 1), [1] * (number_of - 1)
    while spare > 0:
        candidates = [i for i in range(number_of - 1) if counts[i] < bound]
        mass, budget = sum([weights[i] for i in candidates]), spare
        for i in candidates:
            addition = min(bound - counts[i], max(1, budget * weights[i] // mass), spare)
            counts[i] = counts[i] + addition
            spare = spare - addition
    return np.array([bound] + counts)


def ragged(rng, count, total, reach, lean):
    if count == 2:
        one = jax.random.randint(rng, (), max(1, total - reach), min(reach, total - 1) + 1)
        return jnp.stack([one, total - one])
    sizes = jnp.asarray(length_profile(count, total, reach, lean), jnp.int32)
    couples = (count - 1) // 2
    source_of, taker = sizes[1:1 + 2 * couples:2], sizes[2:2 + 2 * couples:2]
    margin = jnp.minimum(source_of - 1, reach - taker)
    moved = jax.random.randint(jax.random.fold_in(rng, 1), (couples,), 0, 1 << 20) % (margin + 1)
    sizes = sizes.at[1:1 + 2 * couples:2].set(source_of - moved).at[2:2 + 2 * couples:2].set(taker + moved)
    return sizes[jax.random.permutation(jax.random.fold_in(rng, 2), count)]


def gaussian(rng, shape, scale, reach, pieces=(), held_as=jnp.bfloat16):
    entries = jax.random.normal(rng, shape, jnp.float32) * scale
    if len(pieces) > 0:
        entries = steps_of(rng, shape, pieces, -0.22, 0.18) * entries
    return jnp.clip(entries, min=-reach, max=reach).astype(held_as)


def setup_inputs(seed: int = 0) -> dict:
    streams_of = jax.random.split(jax.random.key(seed), 13)
    return {
        "tokens": gaussian(streams_of[0], (TOKENS, D), 1.0, 6.0, ((0, 32),)),
        "cotangent": gaussian(streams_of[1], (TOKENS, D), 1.0, 6.0, ((0, 32),)),
        "lengths": jax.vmap(lambda own: ragged(own, NDOC, TOK_DEV, MAXLEN, 2))(jax.random.split(streams_of[2], DEVICES)).reshape((DEVICES, NDOC)).astype(jnp.int32),
        "w_query": gaussian(streams_of[3], (D, D), D ** -0.5, 0.25, ((0, 2),)),
        "w_key": gaussian(streams_of[4], (D, KV), D ** -0.5, 0.25, ((0, 2),)),
        "w_value": gaussian(streams_of[5], (D, KV), D ** -0.5, 0.25, ((0, 2),)),
        "w_out": gaussian(streams_of[6], (D, D), (D // 16) ** -0.5, 1.0, ((0, 2),)),
        "attn_gain": jnp.clip(1.0 + 0.18 * jax.random.normal(streams_of[7], (D,), jnp.float32), 0.099609375, 1.8984375).astype(jnp.bfloat16),
        "w_gate": gaussian(streams_of[8], (D, FF), D ** -0.5, 0.25, ((0, 2),)),
        "w_up": gaussian(streams_of[9], (D, FF), D ** -0.5, 0.25, ((0, 2),)),
        "w_down": gaussian(streams_of[10], (FF, D), (FF // 2) ** -0.5, 0.21875, ((0, 2),)),
        "mlp_gain": jnp.clip(1.0 + 0.18 * jax.random.normal(streams_of[11], (D,), jnp.float32), 0.099609375, 1.8984375).astype(jnp.bfloat16),
    }


@jax.custom_vjp
def low(v):
    return lax.optimization_barrier(v.astype(jnp.bfloat16)).astype(jnp.float32)

@jax.custom_vjp
def low_back(v):
    return v

def low_keep(v):
    return (low(v), None)

def low_pass(kept, grad):
    return (grad,)

def back_keep(v):
    return (v, None)

def back_low(kept, grad):
    return (low(grad),)
low.defvjp(low_keep, low_pass)
low_back.defvjp(back_keep, back_low)
EPS = 1e-05
THETA = 100000.0
HIGH = lax.Precision.HIGHEST

def layout(doc_lengths, count):
    doc_ends = jnp.cumsum(doc_lengths, dtype=jnp.int32)
    doc_starts = doc_ends - doc_lengths
    row_ids = jnp.arange(count, dtype=jnp.int32)
    segment = lax.optimization_barrier(jnp.sum((row_ids[:, None] >= doc_ends[None, :]).astype(jnp.int32), axis=1, dtype=jnp.int32))
    picked = (segment[:, None] == jnp.arange(doc_lengths.shape[0], dtype=jnp.int32)[None, :]).astype(jnp.int32)
    offset = row_ids - lax.optimization_barrier(jnp.sum(picked * doc_starts[None, :], axis=1, dtype=jnp.int32))
    return (segment, offset)

def rotary_tables(offset):
    half_width = HD // 2
    frequency = THETA ** (-2.0 * jnp.arange(half_width, dtype=jnp.float32) / HD)
    angles = offset.astype(jnp.float32)[:, None] * frequency[None, :]
    return (jnp.cos(angles), jnp.sin(angles))

def rotate(values, cosine_part, sine_part):
    count = values.shape[0]
    shaped = values.reshape(count, -1, HD)
    half_width = HD // 2
    front_half = shaped[..., :half_width]
    back_half = shaped[..., half_width:]
    cosine = cosine_part[:, None, :]
    sine_row = sine_part[:, None, :]
    turned = jnp.concatenate([front_half * cosine - back_half * sine_row, back_half * cosine + front_half * sine_row], axis=-1)
    return turned.reshape(count, -1)

def rms_scale(values, gain):
    return values * lax.rsqrt(lax.optimization_barrier(jnp.mean(values * values, axis=-1, keepdims=True)) + EPS) * gain

def allowed_mask(segment, start, block):
    count = segment.shape[0]
    row_ids = start + jnp.arange(block, dtype=jnp.int32)
    columns = jnp.arange(count, dtype=jnp.int32)
    row_segment = lax.dynamic_slice_in_dim(segment, start, block, 0)
    return (row_segment[:, None] == segment[None, :]) & (row_ids[:, None] >= columns[None, :])

def attention(queries, keys, values, segment):
    count = queries.shape[0]
    block = min(512, count)
    groups = H // KVH
    query_heads = queries.reshape(count, KVH, groups, HD)
    key_heads = keys.reshape(count, KVH, HD)
    value_heads = values.reshape(count, KVH, HD)

    def one_block(index):
        start = index * block
        query_block = lax.dynamic_slice_in_dim(query_heads, start, block, 0)
        raw = jnp.einsum('qkgd,tkd->kgqt', query_block, key_heads, precision=HIGH)
        raw = low_back(raw)
        scores = jnp.where(allowed_mask(segment, start, block)[None, None], raw * HD ** (-0.5), -1e+30)
        highest = lax.optimization_barrier(jnp.max(scores, axis=-1, keepdims=True))
        weights = jnp.exp(scores - highest)
        probs = low(weights / lax.optimization_barrier(jnp.sum(weights, axis=-1, keepdims=True)))
        return jnp.einsum('kgqt,tkd->qkgd', probs, value_heads, precision=HIGH)
    blocks = lax.map(jax.checkpoint(one_block), jnp.arange(count // block, dtype=jnp.int32))
    return blocks.reshape(count, H * HD)

def layer(rows_in, doc_lengths, w_query, w_key, w_value, w_out, attn_gain, w_gate, w_up, w_down, mlp_gain):
    count = rows_in.shape[0]
    segment, offset = layout(doc_lengths, count)
    cosine_part, sine_part = rotary_tables(offset)
    normed = low(rms_scale(rows_in, attn_gain))
    q_pre = low_back(jnp.dot(normed, w_query, precision=HIGH))
    k_pre = low_back(jnp.dot(normed, w_key, precision=HIGH))
    v_pre = low_back(jnp.dot(normed, w_value, precision=HIGH))
    queries = low(rotate(q_pre, cosine_part, sine_part))
    keys = low(rotate(k_pre, cosine_part, sine_part))
    values = low(v_pre)
    attended = low(low_back(attention(queries, keys, values, segment)))
    middle = rows_in + low_back(jnp.dot(attended, w_out, precision=HIGH))
    normed_mid = low(rms_scale(middle, mlp_gain))
    gate = low_back(jnp.dot(normed_mid, w_gate, precision=HIGH))
    up_val = low_back(jnp.dot(normed_mid, w_up, precision=HIGH))
    hidden = low(jax.nn.silu(gate) * up_val)
    return middle + low_back(jnp.dot(hidden, w_down, precision=HIGH))

def reference(tokens, cotangent, lengths, w_query, w_key, w_value, w_out, attn_gain, w_gate, w_up, w_down, mlp_gain):
    pack_count = tokens.shape[0] // TOK_DEV

    def forward(act_in, *weights):

        def one_pack(carry, item):
            rows_in, doc_lengths = item
            return (carry, jax.checkpoint(layer)(rows_in, doc_lengths, *weights))
        _, result = lax.scan(one_pack, jnp.zeros((), jnp.float32), (act_in.reshape(pack_count, TOK_DEV, D), lengths))
        return result.reshape(pack_count * TOK_DEV, D)
    floats = [arr.astype(jnp.float32) for arr in (tokens, w_query, w_key, w_value, w_out, attn_gain, w_gate, w_up, w_down, mlp_gain)]
    result, pull = jax.vjp(forward, *floats)
    grads = pull(cotangent.astype(jnp.float32))
    return (result.astype(jnp.bfloat16), grads[0], grads[1], grads[2], grads[3], grads[4], grads[5], grads[6], grads[7], grads[8], grads[9])
```

```python
import functools

import jax
import jax.numpy as jnp
from jax import lax
from jax.experimental import pallas as pl
from jax.experimental.pallas import tpu as pltpu
from jax.sharding import PartitionSpec as P

H = 9
KVH = 3
HD = 64
MAXLEN = 512
EPS = 1e-05
THETA = 100000.0
BLOCK = 256
GROUPS = H // KVH
GQ = GROUPS * HD
GD = GQ + 2 * HD
SCALE = HD ** (-0.5)
F32 = jnp.float32
BF16 = jnp.bfloat16
MIB = 1024 * 1024


def dot_nn(left, right):
    return lax.dot_general(left, right, (((1,), (0,)), ((), ())), preferred_element_type=F32)


def dot_nt(left, right):
    return lax.dot_general(left, right, (((1,), (1,)), ((), ())), preferred_element_type=F32)


def dot_tn(left, right):
    return lax.dot_general(left, right, (((0,), (0,)), ((), ())), preferred_element_type=F32)


def put_rows(full, own, got_a, got_b, shard, core):
    rows = own.shape[0]
    half = rows // 2
    full[pl.ds(pl.multiple_of(shard * rows, 16), rows), :] = own[...]
    other = (1 - shard) * rows
    full[pl.ds(pl.multiple_of(other + core * half, 16), half), :] = got_a[...]
    full[pl.ds(pl.multiple_of(other + (1 - core) * half, 16), half), :] = got_b[...]


def project_kernel(ids, tok, own, got_a, got_b, cos, sin, w_full, normed, q_out, k_out, v_out):
    put_rows(w_full, own, got_a, got_b, ids[0], ids[1])
    width, count = tok.shape
    kv = KVH * HD
    half = HD // 2
    gain = w_full[:, width + 2 * kv : width + 2 * kv + 1].astype(F32)
    for at in range(0, count, BLOCK):
        lanes = slice(at, at + BLOCK)
        x = tok[:, lanes].astype(F32)
        r = lax.rsqrt(jnp.mean(x * x, axis=0, keepdims=True) + EPS)
        normed[:, lanes] = (x * r * gain).astype(BF16)
    for at in range(0, count, BLOCK):
        lanes = slice(at, at + BLOCK)
        pre = dot_tn(w_full[:, : width + 2 * kv], normed[:, lanes])
        c = cos[:, lanes]
        s = sin[:, lanes]
        for head in range(H + KVH):
            row = head * HD
            a = pre[row : row + half]
            b = pre[row + half : row + HD]
            front = a * c - b * s
            back = b * c + a * s
            if head < H:
                q_out[row : row + half, lanes] = (front * SCALE).astype(BF16)
                q_out[row + half : row + HD, lanes] = (back * SCALE).astype(BF16)
            else:
                row -= width
                k_out[row : row + half, lanes] = front.astype(BF16)
                k_out[row + half : row + HD, lanes] = back.astype(BF16)
        v_out[:, lanes] = pre[width + kv :].astype(BF16)


def window(at, blocks, starts):
    low = (at - blocks + 1) * BLOCK
    shape = (blocks * BLOCK, BLOCK)
    rows = low + lax.broadcasted_iota(jnp.int32, shape, 0)
    columns = at * BLOCK + lax.broadcasted_iota(jnp.int32, shape, 1)
    return (rows >= starts) & (rows <= columns)


def reach(at):
    return min(at, (MAXLEN + BLOCK - 2) // BLOCK) + 1


def attend_kernel(need, starts, q, k, v, att, att_low, lse):
    count = q.shape[1]
    k_rows = k[...].T
    for at in range(count // BLOCK):
        lanes = slice(at * BLOCK, (at + 1) * BLOCK)
        for blocks in range(1, reach(at) + 1):

            @pl.when(need[at] == blocks)
            def _(at=at, lanes=lanes, blocks=blocks):
                ok = window(at, blocks, starts[:, lanes])
                span = slice((at - blocks + 1) * BLOCK, (at + 1) * BLOCK)
                for j in range(GROUPS):
                    rows = slice(j * HD, (j + 1) * HD)
                    scores = jnp.where(ok, dot_nn(k_rows[span], q[rows, lanes]), -1e30)
                    top = jnp.max(scores, axis=0, keepdims=True)
                    e = jnp.exp(scores - top)
                    total = jnp.sum(e, axis=0, keepdims=True)
                    o = dot_nn(v[:, span], e.astype(BF16)) / total
                    att[rows, lanes] = o
                    att_low[rows, lanes] = o.astype(BF16)
                    lse[j : j + 1, lanes] = top + jnp.log(total)


def middle_kernel(
    ids, tok, cot, att0, att1, att2, w_full,
    wo_own, wo_a, wo_b, wg_own, wg_a, wg_b, wu_own, wu_a, wu_b, wd_own, wd_a, wd_b,
    out, d_mid, d_att, g_gate_keep, g_gate_send, g_up_keep, g_up_send, g_down_keep, g_down_send,
    g_out_keep, g_out_send,
    wo, wg, wu, wd, nm, low, hid, dg, du,
):
    shard, core = ids[0], ids[1]
    put_rows(wo, wo_own, wo_a, wo_b, shard, core)
    put_rows(wg, wg_own, wg_a, wg_b, shard, core)
    put_rows(wu, wu_own, wu_a, wu_b, shard, core)
    width, count = tok.shape
    hidden = wg.shape[1]
    part = wd_own.shape[1]
    half_rows = width // 2
    for turn in range(2):

        @pl.when(shard == turn)
        def _(turn=turn):
            wd[:, turn * part : (turn + 1) * part] = wd_own[...]
            other = slice((1 - turn) * part, (2 - turn) * part)
            wd[pl.ds(pl.multiple_of(core * half_rows, 16), half_rows), other] = wd_a[...]
            wd[pl.ds(pl.multiple_of((1 - core) * half_rows, 16), half_rows), other] = wd_b[...]

    gain = w_full[:, width + 2 * KVH * HD + 1 : width + 2 * KVH * HD + 2].astype(F32)
    for at in range(0, count, BLOCK):
        lanes = slice(at, at + BLOCK)
        att = jnp.concatenate([att0[:, lanes], att1[:, lanes], att2[:, lanes]], axis=0)
        mid = tok[:, lanes].astype(F32) + dot_tn(wo[...], att)
        r = lax.rsqrt(jnp.mean(mid * mid, axis=0, keepdims=True) + EPS)
        z = mid * r
        nm_part = (z * gain).astype(BF16)
        nm[:, lanes] = nm_part
        nm_rows = nm_part.T
        gate = dot_nn(nm_rows, wg[...])
        up = dot_nn(nm_rows, wu[...])
        sg = jax.nn.sigmoid(gate)
        sw = gate * sg
        hid_part = (sw * up).astype(BF16)
        hid[lanes, :] = hid_part
        out[:, lanes] = (mid + dot_nt(wd[...], hid_part)).astype(BF16)
        cot_part = cot[:, lanes]
        dh = dot_nn(cot_part.T, wd[...])
        dg_part = (dh * up * sg * (1.0 + gate * (1.0 - sg))).astype(BF16)
        du_part = (dh * sw).astype(BF16)
        dg[lanes, :] = dg_part
        du[lanes, :] = du_part
        e = (dot_nt(wg[...], dg_part) + dot_nt(wu[...], du_part)) * gain
        d_part = cot_part.astype(F32) + r * (e - z * jnp.mean(e * z, axis=0, keepdims=True))
        d_mid[:, lanes] = d_part
        low_part = d_part.astype(BF16)
        low[:, lanes] = low_part
        d_att[:, lanes] = dot_nn(wo[...], low_part).astype(BF16)

    quarter = width // 4

    def split(keep, send, x, rows, columns, value):
        for turn in range(2):

            @pl.when(core == turn)
            def _():
                target = keep if rows == turn else send
                target[x, :, columns] = value.astype(BF16)

    step = 384
    for x in range(2):
        for c in range(2):
            first = (2 * x + c) * quarter
            rows = slice(first, first + quarter)
            for at in range(0, hidden, step):
                columns = slice(at, at + step)
                split(g_gate_keep, g_gate_send, x, c, columns, dot_nn(nm[rows, :], dg[:, columns]))
                split(g_up_keep, g_up_send, x, c, columns, dot_nn(nm[rows, :], du[:, columns]))
            for side in range(2):
                first_d = c * half_rows + side * quarter
                for at in range(0, part, step):
                    value = dot_nn(
                        cot[first_d : first_d + quarter, :],
                        hid[:, x * part + at : x * part + at + step],
                    )
                    columns = slice(side * part + at, side * part + at + step)
                    split(g_down_keep, g_down_send, x, c, columns, value)
            left = (att0, att1, att2)
            pieces = []
            for g in range(KVH):
                begin = max(first, g * GQ)
                end = min(first + quarter, (g + 1) * GQ)
                if begin < end:
                    pieces.append(left[g][begin - g * GQ : end - g * GQ, :])
            rows_out = pieces[0] if len(pieces) == 1 else jnp.concatenate(pieces, axis=0)
            split(g_out_keep, g_out_send, x, c, slice(0, width), dot_nt(rows_out, low[...]))


def attend_back_kernel(
    ids, need, starts, q, k, v, d_att, att, lse, cos, sin, normed,
    d_out, g_keep, g_send,
    dk_acc, dv_acc,
):
    count = q.shape[1]
    half = HD // 2
    k_rows = k[...].T
    v_rows = v[...].T
    dk_acc[...] = jnp.zeros_like(dk_acc)
    dv_acc[...] = jnp.zeros_like(dv_acc)
    for at in range(count // BLOCK):
        lanes = slice(at * BLOCK, (at + 1) * BLOCK)
        for blocks in range(1, reach(at) + 1):

            @pl.when(need[at] == blocks)
            def _(at=at, lanes=lanes, blocks=blocks):
                ok = window(at, blocks, starts[:, lanes])
                span = slice((at - blocks + 1) * BLOCK, (at + 1) * BLOCK)
                c = cos[:, lanes]
                s = sin[:, lanes]
                for j in range(GROUPS):
                    rows = slice(j * HD, (j + 1) * HD)
                    q_part = q[rows, lanes]
                    d_part = d_att[rows, lanes]
                    scores = jnp.where(ok, dot_nn(k_rows[span], q_part), -1e30)
                    probs = jnp.exp(scores - lse[j : j + 1, lanes])
                    d_probs = dot_nn(v_rows[span], d_part)
                    centre = jnp.sum(d_part.astype(F32) * att[rows, lanes], axis=0, keepdims=True)
                    d_scores = (probs * (d_probs - centre)).astype(BF16)
                    dq = dot_nn(k[:, span], d_scores) * SCALE
                    a = dq[:half]
                    b = dq[half:]
                    d_out[j * HD : j * HD + half, lanes] = (a * c + b * s).astype(BF16)
                    d_out[j * HD + half : (j + 1) * HD, lanes] = (b * c - a * s).astype(BF16)
                    dk_acc[:, span] += dot_nt(q_part, d_scores)
                    dv_acc[:, span] += dot_nt(d_part, probs.astype(BF16))
    a = dk_acc[:half, :]
    b = dk_acc[half:, :]
    d_out[GQ : GQ + half, :] = (a * cos[...] + b * sin[...]).astype(BF16)
    d_out[GQ + half : GQ + HD, :] = (b * cos[...] - a * sin[...]).astype(BF16)
    d_out[GQ + HD :, :] = dv_acc[...].astype(BF16)
    quarter = normed.shape[0] // 4
    for x in range(2):
        for c in range(2):
            first = (2 * x + c) * quarter
            value = dot_nt(normed[first : first + quarter, :], d_out[...]).astype(BF16)
            for turn in range(2):

                @pl.when(ids[1] == turn)
                def _(turn=turn, c=c, x=x, value=value):
                    target = g_keep if c == turn else g_send
                    target[x, :, :] = value


def input_kernel(tok, d_mid, w_full, d0, d1, d2, d_tok, d_all):
    width, count = tok.shape
    kv = KVH * HD
    for g, part in enumerate((d0, d1, d2)):
        d_all[g * GQ : (g + 1) * GQ, :] = part[:GQ, :]
        d_all[width + g * HD : width + (g + 1) * HD, :] = part[GQ : GQ + HD, :]
        d_all[width + kv + g * HD : width + kv + (g + 1) * HD, :] = part[GQ + HD :, :]
    gain = w_full[:, width + 2 * kv : width + 2 * kv + 1].astype(F32)
    for at in range(0, count, BLOCK):
        lanes = slice(at, at + BLOCK)
        x = tok[:, lanes].astype(F32)
        r = lax.rsqrt(jnp.mean(x * x, axis=0, keepdims=True) + EPS)
        z = x * r
        e = dot_nn(w_full[:, : width + 2 * kv], d_all[:, lanes]) * gain
        d_tok[:, lanes] = d_mid[:, lanes] + r * (e - z * jnp.mean(e * z, axis=0, keepdims=True))


SMEM = pl.BlockSpec(memory_space=pltpu.SMEM)


def vmem(count):
    return [pl.BlockSpec(memory_space=pltpu.VMEM)] * count


def shape(dims, dtype):
    return jax.ShapeDtypeStruct(dims, dtype)


def shards(
    size, tokens, cotangent, lengths, w_query, w_key, w_value, w_out, attn_gain, w_gate, w_up, w_down,
    mlp_gain,
):
    count, width = tokens.shape
    kv = KVH * HD
    rows = w_query.shape[0]
    half = rows // 2
    hidden = w_gate.shape[1]
    part = w_down.shape[0]
    rep = lax.axis_index("rep")
    shard = lax.axis_index("shard")
    core = rep % 2
    ids = jnp.stack([shard, core]).astype(jnp.int32)

    def over_x(value):
        return lax.ppermute(value, "shard", [(0, 1), (1, 0)])

    def over_rep(value, bit):
        return lax.ppermute(value, "rep", [(i, i ^ (1 << bit)) for i in range(size)])

    def pick(value, axis, index, total):
        step = value.shape[axis] // total
        return lax.dynamic_slice_in_dim(value, index * step, step, axis)

    pack = jnp.concatenate(
        [w_query, w_key, w_value, attn_gain[:, None], mlp_gain[:, None], jnp.zeros((rows, 62), BF16)],
        axis=1,
    )
    pack_a = over_x(pick(pack, 0, core, 2))
    pack_b = over_rep(pack_a, 0)
    send = jnp.concatenate([pick(w, 0, core, 2) for w in (w_out, w_gate, w_up)], axis=1)
    send, pack_a = lax.optimization_barrier((send, pack_a))
    mid_a = over_x(send)
    mid_b = over_rep(mid_a, 0)
    down = w_down.T
    send, mid_a = lax.optimization_barrier((pick(down, 0, core, 2), mid_a))
    down_a = over_x(send)
    down_b = over_rep(down_a, 0)

    ends = jnp.cumsum(lengths[0], dtype=jnp.int32)
    begins = ends - lengths[0]
    row_ids = jnp.arange(count, dtype=jnp.int32)
    starts = jnp.max(
        jnp.where(row_ids[None, :] >= begins[:, None], begins[:, None], 0), axis=0
    )
    offset = (row_ids - starts).astype(F32)
    frequency = THETA ** (-2.0 * jnp.arange(HD // 2, dtype=F32) / HD)
    angles = frequency[:, None] * offset[None, :]
    cos = jnp.cos(angles)
    sin = jnp.sin(angles)
    at = jnp.arange(count // BLOCK, dtype=jnp.int32)
    first = jnp.max(jnp.where(at[:, None] * BLOCK >= begins[None, :], begins[None, :], 0), axis=1)
    need = at - first // BLOCK + 1
    starts = starts[None, :]

    params = pltpu.CompilerParams(vmem_limit_bytes=56 * MIB)
    tok = tokens.T
    cot = cotangent.T
    w_full, normed, q, k, v = pl.pallas_call(
        project_kernel,
        out_shape=(
            shape((width, width + 2 * kv + 64), BF16),
            shape((width, count), BF16),
            shape((width, count), BF16),
            shape((kv, count), BF16),
            shape((kv, count), BF16),
        ),
        in_specs=[SMEM] + vmem(6),
        out_specs=vmem(5),
        compiler_params=params,
        cost_estimate=pl.CostEstimate(flops=2 * width * (width + 2 * kv) * count, bytes_accessed=8 * MIB, transcendentals=0),
        name="project",
    )(ids, tok, pack, pack_a, pack_b, cos, sin)

    def one(size_of, index):
        return pl.BlockSpec((size_of, count), lambda i: (index, 0))

    atts, lows, lses = [], [], []
    for g in range(KVH):
        att, low, lse = pl.pallas_call(
            attend_kernel,
            grid=(1,),
            out_shape=(shape((GQ, count), F32), shape((GQ, count), BF16), shape((8, count), F32)),
            in_specs=[SMEM, one(1, 0), one(GQ, g), one(HD, g), one(HD, g)],
            out_specs=(one(GQ, 0), one(GQ, 0), one(8, 0)),
            compiler_params=params,
            cost_estimate=pl.CostEstimate(flops=3 * 10**9, bytes_accessed=2 * MIB, transcendentals=10**6),
            name="attend",
        )(need, starts, q, k, v)
        atts.append(att)
        lows.append(low)
        lses.append(lse)

    wo_cols = slice(0, width)
    wg_cols = slice(width, width + hidden)
    wu_cols = slice(width + hidden, width + 2 * hidden)
    quarter = width // 4
    grads = []
    for columns in (hidden, hidden, hidden, width):
        grads += [shape((2, quarter, columns), BF16)] * 2
    out, d_mid, d_att, *grads = pl.pallas_call(
        middle_kernel,
        out_shape=(
            shape((width, count), BF16),
            shape((width, count), F32),
            shape((width, count), BF16),
            *grads,
        ),
        in_specs=[SMEM] + vmem(18),
        out_specs=vmem(11),
        scratch_shapes=[
            pltpu.VMEM((width, width), BF16),
            pltpu.VMEM((width, hidden), BF16),
            pltpu.VMEM((width, hidden), BF16),
            pltpu.VMEM((width, hidden), BF16),
            pltpu.VMEM((width, count), BF16),
            pltpu.VMEM((width, count), BF16),
            pltpu.VMEM((count, hidden), BF16),
            pltpu.VMEM((count, hidden), BF16),
            pltpu.VMEM((count, hidden), BF16),
        ],
        compiler_params=pltpu.CompilerParams(vmem_limit_bytes=60 * MIB),
        cost_estimate=pl.CostEstimate(flops=20 * 10**9, bytes_accessed=20 * MIB, transcendentals=10**6),
        name="middle",
    )(
        ids, tok, cot, *lows, w_full,
        w_out, mid_a[:, wo_cols], mid_b[:, wo_cols],
        w_gate, mid_a[:, wg_cols], mid_b[:, wg_cols],
        w_up, mid_a[:, wu_cols], mid_b[:, wu_cols],
        down, down_a, down_b,
    )

    bits = max(size.bit_length() - 1, 1)

    def reduce_all(keep, sent, halved):
        total = keep + over_rep(sent, 0)
        total = pick(total, 0, shard, 2)[0] + over_x(pick(total, 0, 1 - shard, 2))[0]
        cuts = []
        for bit in range(1, bits):
            side = (rep >> bit) % 2
            if bit <= halved:
                total = pick(total, 1, side, 2) + over_rep(pick(total, 1, 1 - side, 2), bit)
                cuts.append((bit, side))
            else:
                total = total + over_rep(total, bit)
        for bit, side in reversed(cuts):
            got = over_rep(total, bit)
            total = jnp.where(
                side == 0,
                jnp.concatenate([total, got], axis=1),
                jnp.concatenate([got, total], axis=1),
            )
        got = over_rep(total, 0)
        mine, theirs = total.astype(F32), got.astype(F32)
        return jnp.where(core == 0, mine, theirs), jnp.where(core == 0, theirs, mine)

    gate_0, gate_1 = reduce_all(grads[0], grads[1], 2)
    up_0, up_1 = reduce_all(grads[2], grads[3], 2)
    down_0, down_1 = reduce_all(grads[4], grads[5], 2)
    out_0, out_1 = reduce_all(grads[6], grads[7], 0)

    d_parts, g_parts = [], []
    for g in range(KVH):
        d_part, keep, sent = pl.pallas_call(
            attend_back_kernel,
            grid=(1,),
            out_shape=(
                shape((GD, count), BF16),
                shape((2, quarter, GD), BF16),
                shape((2, quarter, GD), BF16),
            ),
            in_specs=[
                SMEM, SMEM, one(1, 0), one(GQ, g), one(HD, g), one(HD, g), one(GQ, g), one(GQ, 0),
                one(8, 0), one(HD // 2, 0), one(HD // 2, 0), one(width, 0),
            ],
            out_specs=(
                one(GD, 0),
                pl.BlockSpec((2, quarter, GD), lambda i: (0, 0, 0)),
                pl.BlockSpec((2, quarter, GD), lambda i: (0, 0, 0)),
            ),
            scratch_shapes=[pltpu.VMEM((HD, count), F32), pltpu.VMEM((HD, count), F32)],
            compiler_params=params,
            cost_estimate=pl.CostEstimate(flops=8 * 10**9, bytes_accessed=5 * MIB, transcendentals=10**6),
            name="attend_back",
        )(ids, need, starts, q, k, v, d_att, atts[g], lses[g], cos, sin, normed)
        d_parts.append(d_part)
        g_parts.append(reduce_all(keep, sent, 0))

    d_tok = pl.pallas_call(
        input_kernel,
        out_shape=shape((width, count), F32),
        in_specs=vmem(6),
        out_specs=pl.BlockSpec(memory_space=pltpu.VMEM),
        scratch_shapes=[pltpu.VMEM((width + 2 * kv, count), BF16)],
        compiler_params=params,
        cost_estimate=pl.CostEstimate(flops=2 * width * (width + 2 * kv) * count, bytes_accessed=8 * MIB, transcendentals=0),
        name="input_grad",
    )(tok, d_mid, w_full, *d_parts)

    grad_gate = jnp.concatenate([gate_0, gate_1], axis=0)
    grad_up = jnp.concatenate([up_0, up_1], axis=0)
    grad_out = jnp.concatenate([out_0, out_1], axis=0)
    grad_down = jnp.concatenate(
        [down_0[:, :part], down_0[:, part:], down_1[:, :part], down_1[:, part:]], axis=0
    ).T
    whole = [jnp.concatenate(pair, axis=0) for pair in g_parts]
    grad_query = jnp.concatenate([w[:, :GQ] for w in whole], axis=1)
    grad_key = jnp.concatenate([w[:, GQ : GQ + HD] for w in whole], axis=1)
    grad_value = jnp.concatenate([w[:, GQ + HD :] for w in whole], axis=1)

    def along(weight, grad):
        return jnp.sum(weight.astype(F32) * grad, axis=1)

    grad_attn_gain = (
        along(w_query, grad_query) + along(w_key, grad_key) + along(w_value, grad_value)
    ) / attn_gain.astype(F32)
    grad_mlp_gain = (along(w_gate, grad_gate) + along(w_up, grad_up)) / mlp_gain.astype(F32)
    return (
        out.T, d_tok.T, grad_query, grad_key, grad_value, grad_out, grad_attn_gain,
        grad_gate, grad_up, grad_down, grad_mlp_gain,
    )


def solution(mesh):
    everywhere = P(("rep", "shard"), None)
    weight = P("shard", None)
    gain = P("shard")
    return jax.shard_map(
        functools.partial(shards, mesh.shape["rep"]),
        mesh=mesh,
        in_specs=(
            everywhere, everywhere, everywhere, weight, weight, weight, weight, gain, weight, weight,
            weight, gain,
        ),
        out_specs=(
            everywhere, everywhere, weight, weight, weight, weight, gain, weight, weight, weight, gain,
        ),
        check_vma=False,
    )
```

```python
import functools

import jax
import jax.numpy as jnp
from jax import lax
from jax.experimental import pallas as pl
from jax.experimental.pallas import tpu as pltpu
from jax.sharding import PartitionSpec as P

H = 9
KVH = 3
HD = 64
MAXLEN = 512
EPS = 1e-05
THETA = 100000.0
BLOCK = 256
GROUPS = H // KVH
GQ = GROUPS * HD
GD = GQ + 2 * HD
SCALE = HD ** (-0.5)
F32 = jnp.float32
BF16 = jnp.bfloat16
MIB = 1024 * 1024


def dot_nn(left, right):
    return lax.dot_general(left, right, (((1,), (0,)), ((), ())), preferred_element_type=F32)


def dot_nt(left, right):
    return lax.dot_general(left, right, (((1,), (1,)), ((), ())), preferred_element_type=F32)


def dot_tn(left, right):
    return lax.dot_general(left, right, (((0,), (0,)), ((), ())), preferred_element_type=F32)


def put_rows(full, own, got_a, got_b, shard, core):
    rows = own.shape[0]
    half = rows // 2
    full[pl.ds(pl.multiple_of(shard * rows, 16), rows), :] = own[...]
    other = (1 - shard) * rows
    full[pl.ds(pl.multiple_of(other + core * half, 16), half), :] = got_a[...]
    full[pl.ds(pl.multiple_of(other + (1 - core) * half, 16), half), :] = got_b[...]


def pack_first_kernel(ids, wq, wk, wv, attn_gain, mlp_gain, packed):
    rows, width = wq.shape
    part = rows // 2
    half = pl.ds(pl.multiple_of(ids[1] * part, 16), part)
    packed[:part, :width] = wq[half, :]
    packed[:part, width : width + KVH * HD] = wk[half, :]
    packed[:part, width + KVH * HD :] = wv[half, :]
    row = lax.broadcasted_iota(jnp.int32, (packed.shape[0] - part, rows), 0)
    first = attn_gain[...].astype(F32).reshape(1, rows)
    second = mlp_gain[...].astype(F32).reshape(1, rows)
    packed[part:, :rows] = jnp.where(row == 0, first, jnp.where(row == 1, second, 0.0)).astype(BF16)


def pack_rest_kernel(ids, wg, wu, wd, wo, packed_0, packed_1):
    core = ids[1]
    rows = wg.shape[0]
    part = rows // 2
    lane = 128
    shift = wg.shape[1] // 2
    steps = packed_1.shape[1] // (6 * lane)
    half = pl.ds(pl.multiple_of(core * part, 16), part)
    for turn, packed in enumerate((packed_0, packed_1)):
        for step in range(steps):
            low = slice((turn * steps + step) * lane, (turn * steps + step + 1) * lane)
            high = slice(shift + low.start, shift + low.stop)
            to = step * 6 * lane
            for at, (source, columns) in enumerate(((wg, low), (wg, high), (wu, low), (wu, high))):
                packed[:, to + at * lane : to + (at + 1) * lane] = source[half, columns]
            for side in range(2):
                down = pl.ds(pl.multiple_of(core * rows + side * part, 16), part)
                packed[:, to + (4 + side) * lane : to + (5 + side) * lane] = wd[down, low]
    to = steps * 6 * lane
    packed_0[:, to : to + wo.shape[1]] = wo[half, :]


def project_kernel(
    ids, tok, wq, wk, wv, packed, got_a, got_b, cos, sin,
    w_full, gains, normed, q_out, k_out, v_out,
):
    shard, core = ids[0], ids[1]
    rows = wq.shape[0]
    own = pl.ds(pl.multiple_of(shard * rows, 16), rows)
    part = rows // 2
    other = (1 - shard) * rows
    w_full[own, : wq.shape[1]] = wq[...]
    w_full[own, wq.shape[1] : wq.shape[1] + KVH * HD] = wk[...]
    w_full[own, wq.shape[1] + KVH * HD :] = wv[...]
    w_full[pl.ds(pl.multiple_of(other + core * part, 16), part), :] = got_a[:part, :]
    w_full[pl.ds(pl.multiple_of(other + (1 - core) * part, 16), part), :] = got_b[:part, :]
    lanes = (rows + 127) // 128 * 128
    gains[own, :] = packed[part:, :lanes].astype(F32).T[:rows, :8]
    gains[pl.ds(pl.multiple_of(other, 16), rows), :] = got_a[part:, :lanes].astype(F32).T[:rows, :8]
    width, count = tok.shape
    kv = KVH * HD
    half = HD // 2
    gain = gains[:, 0:1]
    for at in range(0, count, BLOCK):
        lanes = slice(at, at + BLOCK)
        x = tok[:, lanes].astype(F32)
        r = lax.rsqrt(jnp.mean(x * x, axis=0, keepdims=True) + EPS)
        normed[:, lanes] = (x * r * gain).astype(BF16)
    for at in range(0, count, BLOCK):
        lanes = slice(at, at + BLOCK)
        pre = dot_tn(w_full[...], normed[:, lanes])
        c = cos[:, lanes]
        s = sin[:, lanes]
        for head in range(H + KVH):
            row = head * HD
            a = pre[row : row + half]
            b = pre[row + half : row + HD]
            front = a * c - b * s
            back = b * c + a * s
            if head < H:
                q_out[row : row + half, lanes] = (front * SCALE).astype(BF16)
                q_out[row + half : row + HD, lanes] = (back * SCALE).astype(BF16)
            else:
                row -= width
                k_out[row : row + half, lanes] = front.astype(BF16)
                k_out[row + half : row + HD, lanes] = back.astype(BF16)
        v_out[:, lanes] = pre[width + kv :].astype(BF16)


def window(at, blocks, starts):
    low = (at - blocks + 1) * BLOCK
    shape = (blocks * BLOCK, BLOCK)
    rows = low + lax.broadcasted_iota(jnp.int32, shape, 0)
    columns = at * BLOCK + lax.broadcasted_iota(jnp.int32, shape, 1)
    return (rows >= starts) & (rows <= columns)


def reach(at):
    return min(at, (MAXLEN + BLOCK - 2) // BLOCK) + 1


def attend_kernel(need, starts, q, k, v, att, att_low, lse):
    count = q.shape[1]
    k_rows = k[...].T
    for at in range(count // BLOCK):
        lanes = slice(at * BLOCK, (at + 1) * BLOCK)
        for blocks in range(1, reach(at) + 1):

            @pl.when(need[at] == blocks)
            def _(at=at, lanes=lanes, blocks=blocks):
                ok = window(at, blocks, starts[:, lanes])
                span = slice((at - blocks + 1) * BLOCK, (at + 1) * BLOCK)
                for j in range(GROUPS):
                    rows = slice(j * HD, (j + 1) * HD)
                    scores = jnp.where(ok, dot_nn(k_rows[span], q[rows, lanes]), -1e30)
                    top = jnp.max(scores, axis=0, keepdims=True)
                    e = jnp.exp(scores - top)
                    total = jnp.sum(e, axis=0, keepdims=True)
                    o = dot_nn(v[:, span], e.astype(BF16)) / total
                    att[rows, lanes] = o
                    att_low[rows, lanes] = o.astype(BF16)
                    lse[j : j + 1, lanes] = top + jnp.log(total)


def split_rows(keep, send, core, x, c, columns, value):
    @pl.when(core == c)
    def _():
        keep[x, :, columns] = value

    @pl.when(core != c)
    def _():
        send[x, :, columns] = value


def hidden_step(
    ids, cot, cot_rows, nm, nm_rows, acc_out, acc_e,
    wg_lo, wg_hi, wu_lo, wu_hi, wd_own, got_a, got_b, keep, send, wg, wu, wd,
):
    shard, core = ids[0], ids[1]
    width = cot.shape[0]
    rows, lane = wg_lo.shape
    half = rows // 2
    own = pl.ds(pl.multiple_of(shard * rows, 16), rows)
    other = (1 - shard) * rows
    at_a = pl.ds(pl.multiple_of(other + core * half, 16), half)
    at_b = pl.ds(pl.multiple_of(other + (1 - core) * half, 16), half)
    wg[own, :lane] = wg_lo[...]
    wg[own, lane:] = wg_hi[...]
    wu[own, :lane] = wu_lo[...]
    wu[own, lane:] = wu_hi[...]
    for at, got in ((at_a, got_a), (at_b, got_b)):
        wg[at, :] = got[:, : 2 * lane]
        wu[at, :] = got[:, 2 * lane : 4 * lane]
    for turn in range(2):

        @pl.when(shard == turn)
        def _(turn=turn):
            wd[:, turn * lane : (turn + 1) * lane] = wd_own[...]
            columns = slice((1 - turn) * lane, (2 - turn) * lane)
            for side in range(2):
                from_a = pl.ds(pl.multiple_of(core * rows + side * half, 16), half)
                from_b = pl.ds(pl.multiple_of((1 - core) * rows + side * half, 16), half)
                source = slice((4 + side) * lane, (5 + side) * lane)
                wd[from_a, columns] = got_a[:, source]
                wd[from_b, columns] = got_b[:, source]

    gate = dot_nn(nm_rows[...], wg[...])
    up = dot_nn(nm_rows[...], wu[...])
    dh = dot_nn(cot_rows[...], wd[...])
    sg = jax.nn.sigmoid(gate)
    sw = gate * sg
    hid = (sw * up).astype(BF16)
    dg = (dh * up * sg * (1.0 + gate * (1.0 - sg))).astype(BF16)
    du = (dh * sw).astype(BF16)
    acc_out[...] += dot_nt(wd[...], hid)
    acc_e[...] += dot_nt(wg[...], dg) + dot_nt(wu[...], du)
    g_gate = dot_nn(nm[...], dg).astype(BF16)
    g_up = dot_nn(nm[...], du).astype(BF16)
    g_down = dot_nn(cot[...], hid).astype(BF16)
    for x in range(2):
        for c in range(2):
            first = (2 * x + c) * half
            split_rows(keep, send, core, x, c, slice(0, 2 * lane), g_gate[first : first + half])
            split_rows(keep, send, core, x, c, slice(2 * lane, 4 * lane), g_up[first : first + half])
            for side in range(2):
                first = c * rows + side * half
                value = g_down[first : first + half, x * lane : (x + 1) * lane]
                columns = slice((4 + side) * lane, (5 + side) * lane)
                split_rows(keep, send, core, x, c, columns, value)


def middle_first_kernel(
    ids, tok, cot, att0, att1, att2, gains, wo_own, wo_a, wo_b,
    wg_lo, wg_hi, wu_lo, wu_hi, wd_own, got_a, got_b,
    mid, nm, acc_out, acc_e, wo, keep, send,
    wg, wu, wd, nm_rows, cot_rows,
):
    @pl.when(pl.program_id(0) == 0)
    def _():
        width = wo.shape[0]
        put_rows(wo, wo_own, wo_a.at[:, :width], wo_b.at[:, :width], ids[0], ids[1])
        gain = gains[:, 1:2]
        att = jnp.concatenate([att0[...], att1[...], att2[...]], axis=0)
        mid[...] = tok[...].astype(F32) + dot_tn(wo[...], att)
        for at in range(0, tok.shape[1], BLOCK):
            lanes = slice(at, at + BLOCK)
            m = mid[:, lanes]
            r = lax.rsqrt(jnp.mean(m * m, axis=0, keepdims=True) + EPS)
            part = (m * r * gain).astype(BF16)
            nm[:, lanes] = part
            nm_rows[lanes, :] = part.T
            cot_rows[lanes, :] = cot[:, lanes].T
        acc_out[...] = mid[...]
        acc_e[...] = jnp.zeros_like(acc_e)

    hidden_step(
        ids, cot, cot_rows, nm, nm_rows, acc_out, acc_e,
        wg_lo, wg_hi, wu_lo, wu_hi, wd_own, got_a, got_b, keep, send, wg, wu, wd,
    )


def middle_second_kernel(
    ids, cot, att0, att1, att2, gains, wo, mid, nm, out_in, e_in,
    wg_lo, wg_hi, wu_lo, wu_hi, wd_own, got_a, got_b,
    out, d_mid, d_att, keep_out, send_out, keep, send,
    wg, wu, wd, nm_rows, cot_rows, acc_out, acc_e,
):
    step = pl.program_id(0)

    @pl.when(step == 0)
    def _():
        for at in range(0, cot.shape[1], BLOCK):
            lanes = slice(at, at + BLOCK)
            nm_rows[lanes, :] = nm[:, lanes].T
            cot_rows[lanes, :] = cot[:, lanes].T
        acc_out[...] = out_in[...]
        acc_e[...] = e_in[...]

    hidden_step(
        ids, cot, cot_rows, nm, nm_rows, acc_out, acc_e,
        wg_lo, wg_hi, wu_lo, wu_hi, wd_own, got_a, got_b, keep, send, wg, wu, wd,
    )

    @pl.when(step == pl.num_programs(0) - 1)
    def _():
        out[...] = acc_out[...].astype(BF16)
        gain = gains[:, 1:2]
        for at in range(0, cot.shape[1], BLOCK):
            lanes = slice(at, at + BLOCK)
            m = mid[:, lanes]
            r = lax.rsqrt(jnp.mean(m * m, axis=0, keepdims=True) + EPS)
            z = m * r
            e = acc_e[:, lanes] * gain
            d_part = cot[:, lanes].astype(F32) + r * (e - z * jnp.mean(e * z, axis=0, keepdims=True))
            d_mid[:, lanes] = d_part
            nm_rows[lanes, :] = d_part.astype(BF16).T
        low = nm_rows[...]
        d_att[...] = dot_nt(wo[...], low).astype(BF16)
        att = jnp.concatenate([att0[...], att1[...], att2[...]], axis=0)
        value = dot_nn(att, low).astype(BF16)
        half = value.shape[0] // 4
        for x in range(2):
            for c in range(2):
                first = (2 * x + c) * half
                split_rows(
                    keep_out, send_out, ids[1], x, c, slice(None), value[first : first + half]
                )


def attend_back_kernel(ids, need, starts, q, k, v, d_att, att, lse, cos, sin, normed, *refs):
    *earlier, d_out, g_keep, g_send, dk_acc, dv_acc = refs
    count = q.shape[1]
    half = HD // 2
    k_rows = k[...].T
    v_rows = v[...].T
    dk_acc[...] = jnp.zeros_like(dk_acc)
    dv_acc[...] = jnp.zeros_like(dv_acc)
    for at in range(count // BLOCK):
        lanes = slice(at * BLOCK, (at + 1) * BLOCK)
        for blocks in range(1, reach(at) + 1):

            @pl.when(need[at] == blocks)
            def _(at=at, lanes=lanes, blocks=blocks):
                ok = window(at, blocks, starts[:, lanes])
                span = slice((at - blocks + 1) * BLOCK, (at + 1) * BLOCK)
                c = cos[:, lanes]
                s = sin[:, lanes]
                for j in range(GROUPS):
                    rows = slice(j * HD, (j + 1) * HD)
                    q_part = q[rows, lanes]
                    d_part = d_att[rows, lanes]
                    scores = jnp.where(ok, dot_nn(k_rows[span], q_part), -1e30)
                    probs = jnp.exp(scores - lse[j : j + 1, lanes])
                    d_probs = dot_nn(v_rows[span], d_part)
                    centre = jnp.sum(d_part.astype(F32) * att[rows, lanes], axis=0, keepdims=True)
                    d_scores = (probs * (d_probs - centre)).astype(BF16)
                    dq = dot_nn(k[:, span], d_scores) * SCALE
                    a = dq[:half]
                    b = dq[half:]
                    d_out[j * HD : j * HD + half, lanes] = (a * c + b * s).astype(BF16)
                    d_out[j * HD + half : (j + 1) * HD, lanes] = (b * c - a * s).astype(BF16)
                    dk_acc[:, span] += dot_nt(q_part, d_scores)
                    dv_acc[:, span] += dot_nt(d_part, probs.astype(BF16))
    a = dk_acc[:half, :]
    b = dk_acc[half:, :]
    d_out[GQ : GQ + half, :] = (a * cos[...] + b * sin[...]).astype(BF16)
    d_out[GQ + half : GQ + HD, :] = (b * cos[...] - a * sin[...]).astype(BF16)
    d_out[GQ + HD :, :] = dv_acc[...].astype(BF16)
    value = dot_nt(normed[...], d_out[...]).astype(BF16)
    quarter = value.shape[0] // 4
    for x in range(2):
        for c in range(2):
            first = (2 * x + c) * quarter
            columns = slice(g_keep.shape[2] - GD, None)
            split_rows(g_keep, g_send, ids[1], x, c, columns, value[first : first + quarter])
    to = 0
    for keep, send in zip(earlier[::2], earlier[1::2]):
        g_keep[:, :, to : to + keep.shape[2]] = keep[...]
        g_send[:, :, to : to + send.shape[2]] = send[...]
        to += keep.shape[2]


def input_kernel(tok, d_mid, w_full, gains, d0, d1, d2, d_tok, d_all):
    width, count = tok.shape
    kv = KVH * HD
    for g, part in enumerate((d0, d1, d2)):
        d_all[g * GQ : (g + 1) * GQ, :] = part[:GQ, :]
        d_all[width + g * HD : width + (g + 1) * HD, :] = part[GQ : GQ + HD, :]
        d_all[width + kv + g * HD : width + kv + (g + 1) * HD, :] = part[GQ + HD :, :]
    gain = gains[:, 0:1]
    for at in range(0, count, BLOCK):
        lanes = slice(at, at + BLOCK)
        x = tok[:, lanes].astype(F32)
        r = lax.rsqrt(jnp.mean(x * x, axis=0, keepdims=True) + EPS)
        z = x * r
        e = dot_nn(w_full[...], d_all[:, lanes]) * gain
        d_tok[:, lanes] = d_mid[:, lanes] + r * (e - z * jnp.mean(e * z, axis=0, keepdims=True))


def row_of(column):
    rows = column.shape[0]
    lanes = (rows + 127) // 128 * 128
    wide = jnp.broadcast_to(column, (rows, 128))
    return jnp.concatenate([wide, jnp.zeros((lanes - rows, 128), F32)], axis=0).T[:8]


def finish_hidden_kernel(ids, mine_1, got_1, mine_2, got_2, wg, wu, gains, gate, up, down, gain_out):
    shard, core = ids[0], ids[1]
    rows, hidden = wg.shape
    half = rows // 2
    lane = 128
    steps = mine_1.shape[1] // (6 * lane)
    sums = []
    for parts, side_of in (((mine_1, mine_2), core), ((got_1, got_2), 1 - core)):
        at = pl.ds(pl.multiple_of(side_of * half, 16), half)
        total = jnp.zeros((half, lane), F32)
        for turn in range(2):
            for step in range(steps):
                low = (turn * steps + step) * lane
                begin = step * 6 * lane
                for high in range(2):
                    columns = slice(high * hidden // 2 + low, high * hidden // 2 + low + lane)
                    g = parts[turn][:, begin + high * lane : begin + (high + 1) * lane].astype(F32)
                    u = parts[turn][:, begin + (2 + high) * lane : begin + (3 + high) * lane].astype(F32)
                    gate[at, columns] = g
                    up[at, columns] = u
                    total += wg[at, columns].astype(F32) * g + wu[at, columns].astype(F32) * u
                for side in range(2):
                    d = parts[turn][:, begin + (4 + side) * lane : begin + (5 + side) * lane]
                    to = pl.ds(pl.multiple_of(side_of * rows + side * half, 16), half)
                    down[to, low : low + lane] = d.astype(F32)
        sums.append((at, jnp.sum(total, axis=1, keepdims=True)))
    own = pl.ds(pl.multiple_of(shard * rows, 16), rows)
    gain = gains[own, 1:2]
    first = jnp.where(core == 0, sums[0][1], sums[1][1])
    second = jnp.where(core == 0, sums[1][1], sums[0][1])
    gain_out[...] = row_of(jnp.concatenate([first, second], axis=0) / gain)


def finish_last_kernel(ids, mine, got, wq, wk, wv, gains, g_out, g_query, g_key, g_value, gain_out):
    shard, core = ids[0], ids[1]
    rows, width = wq.shape
    half = rows // 2
    sums = []
    for part, side_of in ((mine, core), (got, 1 - core)):
        at = pl.ds(pl.multiple_of(side_of * half, 16), half)
        g_out[at, :] = part[:, :width].astype(F32)
        total = jnp.zeros((half, 1), F32)
        for weight, grad, begin, length in (
            (wq, g_query, 0, GQ), (wk, g_key, GQ, HD), (wv, g_value, GQ + HD, HD)
        ):
            pieces = [
                part[:, width + g * GD + begin : width + g * GD + begin + length] for g in range(KVH)
            ]
            value = jnp.concatenate(pieces, axis=1).astype(F32)
            grad[at, :] = value
            total += jnp.sum(weight[at, :].astype(F32) * value, axis=1, keepdims=True)
        sums.append(total)
    own = pl.ds(pl.multiple_of(shard * rows, 16), rows)
    gain = gains[own, 0:1]
    first = jnp.where(core == 0, sums[0], sums[1])
    second = jnp.where(core == 0, sums[1], sums[0])
    gain_out[...] = row_of(jnp.concatenate([first, second], axis=0) / gain)


SMEM = pl.BlockSpec(memory_space=pltpu.SMEM)


def cost(microseconds):
    return pl.CostEstimate(flops=microseconds * 10**9, bytes_accessed=MIB, transcendentals=0)


def vmem(count):
    return [pl.BlockSpec(memory_space=pltpu.VMEM)] * count


def shape(dims, dtype):
    return jax.ShapeDtypeStruct(dims, dtype)


def after(value, *others):
    return lax.optimization_barrier((value, *others))[0]


def shards(
    size, tokens, cotangent, lengths, w_query, w_key, w_value, w_out, attn_gain, w_gate, w_up, w_down,
    mlp_gain,
):
    count, width = tokens.shape
    kv = KVH * HD
    rows = w_query.shape[0]
    quarter = rows // 2
    hidden = w_gate.shape[1]
    part = w_down.shape[0]
    lane = 128
    steps = part // (2 * lane)
    chunk = 6 * lane
    rep = lax.axis_index("rep")
    shard = lax.axis_index("shard")
    core = rep % 2
    ids = jnp.stack([shard, core]).astype(jnp.int32)
    bits = size.bit_length() - 1

    def over_x(value):
        return lax.ppermute(value, "shard", [(0, 1), (1, 0)])

    def over_rep(value, bit):
        return lax.ppermute(value, "rep", [(i, i ^ (1 << bit)) for i in range(size)])

    def pick(value, axis, index, total):
        step = value.shape[axis] // total
        return lax.dynamic_slice_in_dim(value, index * step, step, axis)

    tok = tokens.T
    cot = cotangent.T
    down = w_down.T
    params = pltpu.CompilerParams(vmem_limit_bytes=56 * MIB)
    packed = pl.pallas_call(
        pack_first_kernel,
        out_shape=shape((quarter + 16, width + 2 * kv), BF16),
        in_specs=[SMEM] + vmem(5),
        out_specs=pl.BlockSpec(memory_space=pltpu.VMEM),
        cost_estimate=cost(2),
        name="pack_first",
    )(ids, w_query, w_key, w_value, attn_gain, mlp_gain)
    second, third = pl.pallas_call(
        pack_rest_kernel,
        out_shape=(
            shape((quarter, (steps + 1) * chunk), BF16),
            shape((quarter, steps * chunk), BF16),
        ),
        in_specs=[SMEM] + vmem(4),
        out_specs=vmem(2),
        compiler_params=params,
        cost_estimate=cost(3),
        name="pack_rest",
    )(after(ids, packed), w_gate, w_up, down, w_out)
    first_a = after(over_x(packed), second)
    first_b = over_rep(first_a, 0)
    second = after(second, first_a)

    ends = jnp.cumsum(lengths[0], dtype=jnp.int32)
    begins = ends - lengths[0]
    row_ids = jnp.arange(count, dtype=jnp.int32)
    starts = jnp.max(jnp.where(row_ids[None, :] >= begins[:, None], begins[:, None], 0), axis=0)
    offset = (row_ids - starts).astype(F32)
    frequency = THETA ** (-2.0 * jnp.arange(HD // 2, dtype=F32) / HD)
    angles = frequency[:, None] * offset[None, :]
    cos = jnp.cos(angles)
    sin = jnp.sin(angles)
    at = jnp.arange(count // BLOCK, dtype=jnp.int32)
    first = jnp.max(jnp.where(at[:, None] * BLOCK >= begins[None, :], begins[None, :], 0), axis=1)
    need = at - first // BLOCK + 1
    starts = starts[None, :]

    w_full, gains, normed, q, k, v = pl.pallas_call(
        project_kernel,
        out_shape=(
            shape((width, width + 2 * kv), BF16),
            shape((width, 8), F32),
            shape((width, count), BF16),
            shape((width, count), BF16),
            shape((kv, count), BF16),
            shape((kv, count), BF16),
        ),
        in_specs=[SMEM] + vmem(9),
        out_specs=vmem(6),
        compiler_params=params,
        cost_estimate=cost(5),
        name="project",
    )(after(ids, second), tok, w_query, w_key, w_value, packed, first_a, first_b, cos, sin)

    def one(size_of, index):
        return pl.BlockSpec((size_of, count), lambda i: (index, 0))

    atts, lows, lses = [], [], []
    for g in range(KVH):
        if g == KVH - 1:
            second_a = after(over_x(second), lses[-1])
            third = after(third, second_a)
        att, low, lse = pl.pallas_call(
            attend_kernel,
            grid=(1,),
            out_shape=(shape((GQ, count), F32), shape((GQ, count), BF16), shape((8, count), F32)),
            in_specs=[SMEM, one(1, 0), one(GQ, g), one(HD, g), one(HD, g)],
            out_specs=(one(GQ, 0), one(GQ, 0), one(8, 0)),
            compiler_params=params,
            cost_estimate=cost(7),
            name="attend",
        )(after(need, *lses[-1:], *([third] if g == KVH - 1 else [])), starts, q, k, v)
        atts.append(att)
        lows.append(low)
        lses.append(lse)

    second_b = after(over_rep(second_a, 0), lses[-1])

    def whole(dims):
        return pl.BlockSpec(dims, lambda i: (0,) * len(dims))

    def hidden_specs(turn):
        low = pl.BlockSpec((rows, lane), lambda i: (0, turn * steps + i))
        high = pl.BlockSpec((rows, lane), lambda i: (0, (2 + turn) * steps + i))
        return [
            low, high, low, high,
            pl.BlockSpec((width, lane), lambda i: (0, turn * steps + i)),
            pl.BlockSpec((quarter, chunk), lambda i: (0, i)),
            pl.BlockSpec((quarter, chunk), lambda i: (0, i)),
        ]

    wide = whole((width, count))
    att_specs = [whole((GQ, count))] * KVH
    grad_spec = pl.BlockSpec((2, quarter, chunk), lambda i: (0, 0, i))
    grad_shape = shape((2, quarter, chunk * steps), BF16)
    weight_scratch = [pltpu.VMEM((width, 2 * lane), BF16)] * 3 + [pltpu.VMEM((count, width), BF16)] * 2
    wo_spec = pl.BlockSpec((quarter, chunk), lambda i: (0, steps))
    mid, nm, acc_out, acc_e, wo, keep_1, send_1 = pl.pallas_call(
        middle_first_kernel,
        grid=(steps,),
        out_shape=(
            shape((width, count), F32),
            shape((width, count), BF16),
            shape((width, count), F32),
            shape((width, count), F32),
            shape((width, width), BF16),
            grad_shape,
            grad_shape,
        ),
        in_specs=[SMEM, wide, wide] + att_specs
        + [whole((width, 8)), whole((rows, width)), wo_spec, wo_spec] + hidden_specs(0),
        out_specs=(wide, wide, wide, wide, whole((width, width)), grad_spec, grad_spec),
        scratch_shapes=weight_scratch,
        compiler_params=params,
        cost_estimate=cost(18),
        name="middle_first",
    )(
        ids, tok, cot, *lows, gains, w_out, second_a, second_b,
        w_gate, w_gate, w_up, w_up, down, second_a, second_b,
    )

    def scatter_x(total):
        return pick(total, 0, shard, 2)[0], pick(total, 0, 1 - shard, 2)[0]

    def half_of(total, bit, axis):
        side = (rep >> bit) % 2
        return pick(total, axis, side, 2), pick(total, axis, 1 - side, 2)

    def join(total, got, bit, axis):
        side = (rep >> bit) % 2
        return jnp.where(
            side == 0,
            jnp.concatenate([total, got], axis=axis),
            jnp.concatenate([got, total], axis=axis),
        )

    def reduce_steps(keep, send, cuts):
        def end(value, marker):
            return value if marker is None else after(value, marker)

        sent = send
        marker = yield sent
        total = keep + end(over_rep(sent, 0), marker)
        stay, sent = scatter_x(total)
        marker = yield sent
        total = stay + end(over_x(sent), marker)
        done = []
        for bit in range(1, bits):
            if bit in cuts:
                stay, sent = half_of(total, bit, cuts[bit])
                done.append(bit)
            else:
                stay = sent = total
            marker = yield sent
            total = stay + end(over_rep(sent, bit), marker)
        for bit in reversed(done):
            marker = yield total
            total = join(total, end(over_rep(total, bit), marker), bit, cuts[bit])
        marker = yield total
        yield total, end(over_rep(total, 0), marker)

    third_a = after(over_x(third), mid)
    third_b = over_rep(third_a, 0)
    run_1 = reduce_steps(keep_1, after(send_1, third_a), {1: 0, 2: 1})
    next(run_1)
    out, d_mid, d_att, keep_o, send_o, keep_2, send_2 = pl.pallas_call(
        middle_second_kernel,
        grid=(steps,),
        out_shape=(
            shape((width, count), BF16),
            shape((width, count), F32),
            shape((width, count), BF16),
            shape((2, quarter, width), BF16),
            shape((2, quarter, width), BF16),
            grad_shape,
            grad_shape,
        ),
        in_specs=[SMEM, wide] + att_specs
        + [whole((width, 8)), whole((width, width)), wide, wide, wide, wide] + hidden_specs(1),
        out_specs=(
            wide, wide, wide, whole((2, quarter, width)), whole((2, quarter, width)),
            grad_spec, grad_spec,
        ),
        scratch_shapes=weight_scratch
        + [pltpu.VMEM((width, count), F32), pltpu.VMEM((width, count), F32)],
        compiler_params=params,
        cost_estimate=cost(18),
        name="middle_second",
    )(
        after(ids, run_1.send(None)), cot, *lows, gains, wo, mid, nm, acc_out, acc_e,
        w_gate, w_gate, w_up, w_up, down, third_a, third_b,
    )
    run_2 = reduce_steps(keep_2, send_2, {1: 0, 2: 1})
    next(run_2)
    sent = [run_1.send(d_mid), run_2.send(None)]

    d_parts, earlier = [], [keep_o, send_o]
    for g in range(KVH):
        joined = earlier if g == KVH - 1 else []
        grads_to = (2, quarter, GD + sum(x.shape[2] for x in joined[::2]))
        d_part, *pair = pl.pallas_call(
            attend_back_kernel,
            grid=(1,),
            out_shape=(
                shape((GD, count), BF16),
                shape(grads_to, BF16),
                shape(grads_to, BF16),
            ),
            in_specs=[
                SMEM, SMEM, one(1, 0), one(GQ, g), one(HD, g), one(HD, g), one(GQ, g), one(GQ, 0),
                one(8, 0), one(HD // 2, 0), one(HD // 2, 0), one(width, 0),
            ] + [whole(x.shape) for x in joined],
            out_specs=(one(GD, 0), whole(grads_to), whole(grads_to)),
            scratch_shapes=[pltpu.VMEM((HD, count), F32), pltpu.VMEM((HD, count), F32)],
            compiler_params=params,
            cost_estimate=cost(10),
            name="attend_back",
        )(
            after(ids, *sent), need, starts, q, k, v, d_att, atts[g], lses[g],
            cos, sin, normed, *joined,
        )
        d_parts.append(d_part)
        earlier += pair
        sent = [run_1.send(d_part), run_2.send(d_part)]
    run_3 = reduce_steps(pair[0], after(pair[1], *sent), {1: 1})
    next(run_3)
    sent.append(run_3.send(None))

    d_tok = pl.pallas_call(
        input_kernel,
        out_shape=shape((width, count), F32),
        in_specs=vmem(7),
        out_specs=pl.BlockSpec(memory_space=pltpu.VMEM),
        scratch_shapes=[pltpu.VMEM((width + 2 * kv, count), BF16)],
        compiler_params=params,
        cost_estimate=cost(7),
        name="input_grad",
    )(after(tok, *sent), d_mid, w_full, gains, *d_parts)

    for run in (run_1, run_2, run_3):
        sent = run.send(d_tok)

    def last(run):
        for value in run:
            pass
        return value

    for bit in range(2, bits):
        sent = run_3.send(None)
    sent = run_3.send(None)
    parts_1, parts_2 = last(run_1), last(run_2)
    gain_shape = shape((8, (rows + 127) // 128 * 128), F32)
    grad_gate, grad_up, grad_down, grad_mlp_gain = pl.pallas_call(
        finish_hidden_kernel,
        out_shape=(
            shape((rows, hidden), F32), shape((rows, hidden), F32), shape((width, part), F32), gain_shape
        ),
        in_specs=[SMEM] + vmem(7),
        out_specs=vmem(4),
        compiler_params=params,
        cost_estimate=cost(5),
        name="finish_hidden",
    )(after(ids, sent), *parts_1, *parts_2, w_gate, w_up, gains)
    run_3.send(grad_mlp_gain)
    grad_out, grad_query, grad_key, grad_value, grad_attn_gain = pl.pallas_call(
        finish_last_kernel,
        out_shape=(
            shape((rows, width), F32), shape((rows, width), F32), shape((rows, kv), F32),
            shape((rows, kv), F32), gain_shape,
        ),
        in_specs=[SMEM] + vmem(6),
        out_specs=vmem(5),
        compiler_params=params,
        cost_estimate=cost(3),
        name="finish_last",
    )(ids, *last(run_3), w_query, w_key, w_value, gains)
    grad_down = grad_down.T
    grad_mlp_gain = grad_mlp_gain[0, :rows]
    grad_attn_gain = grad_attn_gain[0, :rows]
    return (
        out.T, d_tok.T, grad_query, grad_key, grad_value, grad_out, grad_attn_gain,
        grad_gate, grad_up, grad_down, grad_mlp_gain,
    )


def solution(mesh):
    everywhere = P(("rep", "shard"), None)
    weight = P("shard", None)
    gain = P("shard")
    return jax.shard_map(
        functools.partial(shards, mesh.shape["rep"]),
        mesh=mesh,
        in_specs=(
            everywhere, everywhere, everywhere, weight, weight, weight, weight, gain, weight, weight,
            weight, gain,
        ),
        out_specs=(
            everywhere, everywhere, weight, weight, weight, weight, gain, weight, weight, weight, gain,
        ),
        check_vma=False,
    )
```

```python
import functools

import jax
import jax.numpy as jnp
from jax import lax
from jax.experimental import pallas as pl
from jax.experimental.pallas import tpu as pltpu
from jax.sharding import PartitionSpec as P

H = 9
KVH = 3
HD = 64
MAXLEN = 512
EPS = 1e-05
THETA = 100000.0
BLOCK = 256
STRIP = 128
GROUPS = H // KVH
GQ = GROUPS * HD
GD = GQ + 2 * HD
SCALE = HD ** (-0.5)
F32 = jnp.float32
BF16 = jnp.bfloat16
MIB = 1024 * 1024


def dot_nn(left, right):
    return lax.dot_general(left, right, (((1,), (0,)), ((), ())), preferred_element_type=F32)


def dot_nt(left, right):
    return lax.dot_general(left, right, (((1,), (1,)), ((), ())), preferred_element_type=F32)


def dot_tn(left, right):
    return lax.dot_general(left, right, (((0,), (0,)), ((), ())), preferred_element_type=F32)


def put_rows(full, own, got_a, got_b, shard, core):
    rows = own.shape[0]
    half = rows // 2
    full[pl.ds(pl.multiple_of(shard * rows, 16), rows), :] = own[...]
    other = (1 - shard) * rows
    full[pl.ds(pl.multiple_of(other + core * half, 16), half), :] = got_a[...]
    full[pl.ds(pl.multiple_of(other + (1 - core) * half, 16), half), :] = got_b[...]


def pack_first_kernel(ids, wq, wk, wv, attn_gain, mlp_gain, packed):
    rows, width = wq.shape
    part = rows // 2
    half = pl.ds(pl.multiple_of(ids[1] * part, 16), part)
    packed[:part, :width] = wq[half, :]
    packed[:part, width : width + KVH * HD] = wk[half, :]
    packed[:part, width + KVH * HD :] = wv[half, :]
    row = lax.broadcasted_iota(jnp.int32, (packed.shape[0] - part, rows), 0)
    first = attn_gain[...].astype(F32).reshape(1, rows)
    second = mlp_gain[...].astype(F32).reshape(1, rows)
    packed[part:, :rows] = jnp.where(row == 0, first, jnp.where(row == 1, second, 0.0)).astype(BF16)


def pack_rest_kernel(ids, wg, wu, wd, wo, packed_0, packed_1):
    core = ids[1]
    rows = wg.shape[0]
    part = rows // 2
    lane = 128
    shift = wg.shape[1] // 2
    steps = packed_1.shape[1] // (6 * lane)
    first = shift // lane - steps
    half = pl.ds(pl.multiple_of(core * part, 16), part)
    for packed, begin, end in ((packed_0, 0, first), (packed_1, first, first + steps)):
        for step in range(begin, end):
            low = slice(step * lane, (step + 1) * lane)
            high = slice(shift + low.start, shift + low.stop)
            to = (step - begin) * 6 * lane
            for at, (source, columns) in enumerate(((wg, low), (wg, high), (wu, low), (wu, high))):
                packed[:, to + at * lane : to + (at + 1) * lane] = source[half, columns]
            for side in range(2):
                down = pl.ds(pl.multiple_of(core * rows + side * part, 16), part)
                packed[:, to + (4 + side) * lane : to + (5 + side) * lane] = wd[down, low]
    to = first * 6 * lane
    packed_0[:, to : to + wo.shape[1]] = wo[half, :]


def project_kernel(
    ids, tok, wq, wk, wv, packed, got_a, got_b, cos, sin,
    w_full, gains, normed, q_out, k_out, v_out,
):
    shard, core = ids[0], ids[1]
    rows = wq.shape[0]
    own = pl.ds(pl.multiple_of(shard * rows, 16), rows)
    part = rows // 2
    other = (1 - shard) * rows
    w_full[own, : wq.shape[1]] = wq[...]
    w_full[own, wq.shape[1] : wq.shape[1] + KVH * HD] = wk[...]
    w_full[own, wq.shape[1] + KVH * HD :] = wv[...]
    w_full[pl.ds(pl.multiple_of(other + core * part, 16), part), :] = got_a[:part, :]
    w_full[pl.ds(pl.multiple_of(other + (1 - core) * part, 16), part), :] = got_b[:part, :]
    lanes = (rows + 127) // 128 * 128
    gains[own, :] = packed[part:, :lanes].astype(F32).T[:rows, :8]
    gains[pl.ds(pl.multiple_of(other, 16), rows), :] = got_a[part:, :lanes].astype(F32).T[:rows, :8]
    width, count = tok.shape
    kv = KVH * HD
    half = HD // 2
    gain = gains[:, 0:1]
    for at in range(0, count, BLOCK):
        lanes = slice(at, at + BLOCK)
        x = tok[:, lanes].astype(F32)
        r = lax.rsqrt(jnp.mean(x * x, axis=0, keepdims=True) + EPS)
        normed[:, lanes] = (x * r * gain).astype(BF16)
    for at in range(0, count, BLOCK):
        lanes = slice(at, at + BLOCK)
        pre = dot_tn(w_full[...], normed[:, lanes])
        c = cos[:, lanes]
        s = sin[:, lanes]
        for head in range(H + KVH):
            row = head * HD
            a = pre[row : row + half]
            b = pre[row + half : row + HD]
            front = a * c - b * s
            back = b * c + a * s
            if head < H:
                q_out[row : row + half, lanes] = (front * SCALE).astype(BF16)
                q_out[row + half : row + HD, lanes] = (back * SCALE).astype(BF16)
            else:
                row -= width
                k_out[row : row + half, lanes] = front.astype(BF16)
                k_out[row + half : row + HD, lanes] = back.astype(BF16)
        v_out[:, lanes] = pre[width + kv :].astype(BF16)


def side_by_side(ref, lanes, rows=HD):
    return jnp.concatenate([ref[j * rows : (j + 1) * rows, lanes] for j in range(GROUPS)], axis=1)


def span_of(at, strips):
    return slice((at + 1) * BLOCK - strips * STRIP, (at + 1) * BLOCK)


def window(at, strips, starts):
    rows = lax.broadcasted_iota(jnp.int32, (strips * STRIP, GROUPS * BLOCK), 0)
    rows += span_of(at, strips).start
    columns = at * BLOCK + lax.broadcasted_iota(jnp.int32, (1, BLOCK), 1)
    starts = jnp.concatenate([starts] * GROUPS, axis=1)
    columns = jnp.concatenate([columns] * GROUPS, axis=1)
    return (rows >= starts) & (rows <= columns)


def reaches(at):
    own = BLOCK // STRIP
    return range(own, min((at + 1) * own, own + (MAXLEN + STRIP - 2) // STRIP) + 1)


def attend_kernel(need, starts, q, k, v, att, att_low, lse):
    count = q.shape[1]
    k_rows = k[...].T
    for at in range(count // BLOCK):
        lanes = slice(at * BLOCK, (at + 1) * BLOCK)
        for strips in reaches(at):

            @pl.when(need[at] == strips)
            def _(at=at, lanes=lanes, strips=strips):
                ok = window(at, strips, starts[:, lanes])
                span = span_of(at, strips)
                scores = jnp.where(ok, dot_nn(k_rows[span], side_by_side(q, lanes)), -1e30)
                top = jnp.max(scores, axis=0, keepdims=True)
                e = jnp.exp(scores - top)
                total = jnp.sum(e, axis=0, keepdims=True)
                o = dot_nn(v[:, span], e.astype(BF16)) / total
                logs = top + jnp.log(total)
                for j in range(GROUPS):
                    rows = slice(j * HD, (j + 1) * HD)
                    one = slice(j * BLOCK, (j + 1) * BLOCK)
                    att[rows, lanes] = o[:, one]
                    att_low[rows, lanes] = o[:, one].astype(BF16)
                    lse[j : j + 1, lanes] = logs[:, one]


def split_rows(keep, send, core, x, c, columns, value):
    @pl.when(core == c)
    def _():
        keep[x, :, columns] = value

    @pl.when(core != c)
    def _():
        send[x, :, columns] = value


def hidden_step(
    ids, cot, cot_rows, nm, nm_rows, acc_out, acc_e,
    wg_lo, wg_hi, wu_lo, wu_hi, wd_own, got_a, got_b, keep, send, wg, wu, wd, base,
):
    shard, core = ids[0], ids[1]
    width = cot.shape[0]
    rows, lane = wg_lo.shape
    half = rows // 2
    own = pl.ds(pl.multiple_of(shard * rows, 16), rows)
    other = (1 - shard) * rows
    at_a = pl.ds(pl.multiple_of(other + core * half, 16), half)
    at_b = pl.ds(pl.multiple_of(other + (1 - core) * half, 16), half)
    wg[own, :lane] = wg_lo[...]
    wg[own, lane:] = wg_hi[...]
    wu[own, :lane] = wu_lo[...]
    wu[own, lane:] = wu_hi[...]
    for at, got in ((at_a, got_a), (at_b, got_b)):
        wg[at, :] = got[:, : 2 * lane]
        wu[at, :] = got[:, 2 * lane : 4 * lane]
    for turn in range(2):

        @pl.when(shard == turn)
        def _(turn=turn):
            wd[:, turn * lane : (turn + 1) * lane] = wd_own[...]
            columns = slice((1 - turn) * lane, (2 - turn) * lane)
            for side in range(2):
                from_a = pl.ds(pl.multiple_of(core * rows + side * half, 16), half)
                from_b = pl.ds(pl.multiple_of((1 - core) * rows + side * half, 16), half)
                source = slice((4 + side) * lane, (5 + side) * lane)
                wd[from_a, columns] = got_a[:, source]
                wd[from_b, columns] = got_b[:, source]

    gate = dot_nn(nm_rows[...], wg[...])
    up = dot_nn(nm_rows[...], wu[...])
    dh = dot_nn(cot_rows[...], wd[...])
    sg = jax.nn.sigmoid(gate)
    sw = gate * sg
    hid = (sw * up).astype(BF16)
    dg = (dh * up * sg * (1.0 + gate * (1.0 - sg))).astype(BF16)
    du = (dh * sw).astype(BF16)
    acc_out[...] += dot_nt(wd[...], hid)
    acc_e[...] += dot_nt(wg[...], dg) + dot_nt(wu[...], du)
    g_gate = dot_nn(nm[...], dg).astype(BF16)
    g_up = dot_nn(nm[...], du).astype(BF16)
    g_down = dot_nn(cot[...], hid).astype(BF16)
    for x in range(2):
        for c in range(2):
            first = (2 * x + c) * half
            at_gate = pl.ds(pl.multiple_of(base, lane), 2 * lane)
            at_up = pl.ds(pl.multiple_of(base + 2 * lane, lane), 2 * lane)
            split_rows(keep, send, core, x, c, at_gate, g_gate[first : first + half])
            split_rows(keep, send, core, x, c, at_up, g_up[first : first + half])
            for side in range(2):
                first = c * rows + side * half
                value = g_down[first : first + half, x * lane : (x + 1) * lane]
                columns = pl.ds(pl.multiple_of(base + (4 + side) * lane, lane), lane)
                split_rows(keep, send, core, x, c, columns, value)


def middle_first_kernel(
    ids, tok, cot, att0, att1, att2, gains, wo_own, wo_a, wo_b,
    wg_lo, wg_hi, wu_lo, wu_hi, wd_own, got_a, got_b,
    mid_out, nm_out, acc_out, acc_e, wo_out, keep, send,
    wg, wu, wd, nm_rows, cot_rows, mid, nm, wo, sems,
):
    step = pl.program_id(0)
    copies = [
        pltpu.make_async_copy(source, target, sems.at[at])
        for at, (source, target) in enumerate(((mid, mid_out), (nm, nm_out), (wo, wo_out)))
    ]

    @pl.when(step == 0)
    def _():
        width = wo.shape[0]
        put_rows(wo, wo_own, wo_a.at[:, :width], wo_b.at[:, :width], ids[0], ids[1])
        copies[2].start()
        gain = gains[:, 1:2]
        att = jnp.concatenate([att0[...], att1[...], att2[...]], axis=0)
        mid[...] = tok[...].astype(F32) + dot_tn(wo[...], att)
        copies[0].start()
        for at in range(0, tok.shape[1], BLOCK):
            lanes = slice(at, at + BLOCK)
            m = mid[:, lanes]
            r = lax.rsqrt(jnp.mean(m * m, axis=0, keepdims=True) + EPS)
            part = (m * r * gain).astype(BF16)
            nm[:, lanes] = part
            nm_rows[lanes, :] = part.T
            cot_rows[lanes, :] = cot[:, lanes].T
        copies[1].start()
        acc_out[...] = jnp.zeros_like(acc_out)
        acc_e[...] = jnp.zeros_like(acc_e)

    hidden_step(
        ids, cot, cot_rows, nm, nm_rows, acc_out, acc_e,
        wg_lo, wg_hi, wu_lo, wu_hi, wd_own, got_a, got_b, keep, send, wg, wu, wd, 0,
    )

    @pl.when(step == pl.num_programs(0) - 1)
    def _():
        for copy in copies:
            copy.wait()


def middle_second_kernel(
    ids, cot, nm, gains, att0, att1, att2, wo_in, mid_in, out_in, e_in,
    wg_lo, wg_hi, wu_lo, wu_hi, wd_own, got_a, got_b,
    out_out, d_mid_out, d_att_out, keep, send,
    wg, wu, wd, nm_rows, cot_rows, acc_out, acc_e, att, wo, mid, out_first, e_first, out, d_att, sems,
):
    step = pl.program_id(0)
    rows = att0.shape[0]
    arrive = [
        (att0, att.at[:rows, :]), (att1, att.at[rows : 2 * rows, :]), (att2, att.at[2 * rows :, :]),
        (wo_in, wo), (mid_in, mid), (out_in, out_first), (e_in, e_first),
    ]
    arrive = [pltpu.make_async_copy(*pair, sems.at[at]) for at, pair in enumerate(arrive)]
    leave = [(out, out_out), (mid, d_mid_out), (d_att, d_att_out)]
    leave = [pltpu.make_async_copy(*pair, sems.at[7 + at]) for at, pair in enumerate(leave)]

    @pl.when(step == 0)
    def _():
        for copy in arrive:
            copy.start()
        for at in range(0, cot.shape[1], BLOCK):
            lanes = slice(at, at + BLOCK)
            nm_rows[lanes, :] = nm[:, lanes].T
            cot_rows[lanes, :] = cot[:, lanes].T
        acc_out[...] = jnp.zeros_like(acc_out)
        acc_e[...] = jnp.zeros_like(acc_e)

    hidden_step(
        ids, cot, cot_rows, nm, nm_rows, acc_out, acc_e,
        wg_lo, wg_hi, wu_lo, wu_hi, wd_own, got_a, got_b, keep, send, wg, wu, wd,
        step * (6 * wg_lo.shape[1]),
    )

    @pl.when(step == pl.num_programs(0) - 1)
    def _():
        for copy in arrive:
            copy.wait()
        out[...] = (mid[...] + out_first[...] + acc_out[...]).astype(BF16)
        leave[0].start()
        gain = gains[:, 1:2]
        for at in range(0, cot.shape[1], BLOCK):
            lanes = slice(at, at + BLOCK)
            m = mid[:, lanes]
            r = lax.rsqrt(jnp.mean(m * m, axis=0, keepdims=True) + EPS)
            z = m * r
            e = (e_first[:, lanes] + acc_e[:, lanes]) * gain
            d_part = cot[:, lanes].astype(F32) + r * (e - z * jnp.mean(e * z, axis=0, keepdims=True))
            mid[:, lanes] = d_part
            nm_rows[lanes, :] = d_part.astype(BF16).T
        leave[1].start()
        low = nm_rows[...]
        d_att[...] = dot_nt(wo[...], low).astype(BF16)
        leave[2].start()
        value = dot_nn(att[...], low).astype(BF16)
        half = value.shape[0] // 4
        done = pl.num_programs(0) * 6 * wg_lo.shape[1]
        for x in range(2):
            for c in range(2):
                first = (2 * x + c) * half
                columns = slice(done, done + value.shape[1])
                split_rows(keep, send, ids[1], x, c, columns, value[first : first + half])
        for copy in leave:
            copy.wait()


def attend_back_kernel(ids, need, starts, q, k, v, d_att, att, lse, cos, sin, normed, *refs):
    *earlier, d_out, g_keep, g_send, dk_acc, dv_acc = refs
    count = q.shape[1]
    half = HD // 2
    k_rows = k[...].T
    v_rows = v[...].T
    dk_acc[...] = jnp.zeros_like(dk_acc)
    dv_acc[...] = jnp.zeros_like(dv_acc)
    for at in range(count // BLOCK):
        lanes = slice(at * BLOCK, (at + 1) * BLOCK)
        for strips in reaches(at):

            @pl.when(need[at] == strips)
            def _(at=at, lanes=lanes, strips=strips):
                ok = window(at, strips, starts[:, lanes])
                span = span_of(at, strips)
                c = cos[:, lanes]
                s = sin[:, lanes]
                q_part = side_by_side(q, lanes)
                d_part = side_by_side(d_att, lanes)
                scores = jnp.where(ok, dot_nn(k_rows[span], q_part), -1e30)
                probs = jnp.exp(scores - side_by_side(lse, lanes, 1))
                d_probs = dot_nn(v_rows[span], d_part)
                centre = jnp.sum(
                    d_part.astype(F32) * side_by_side(att, lanes), axis=0, keepdims=True
                )
                d_scores = (probs * (d_probs - centre)).astype(BF16)
                dq = dot_nn(k[:, span], d_scores) * SCALE
                for j in range(GROUPS):
                    one = slice(j * BLOCK, (j + 1) * BLOCK)
                    a = dq[:half, one]
                    b = dq[half:, one]
                    d_out[j * HD : j * HD + half, lanes] = (a * c + b * s).astype(BF16)
                    d_out[j * HD + half : (j + 1) * HD, lanes] = (b * c - a * s).astype(BF16)
                dk_acc[:, span] += dot_nt(q_part, d_scores)
                dv_acc[:, span] += dot_nt(d_part, probs.astype(BF16))
    a = dk_acc[:half, :]
    b = dk_acc[half:, :]
    d_out[GQ : GQ + half, :] = (a * cos[...] + b * sin[...]).astype(BF16)
    d_out[GQ + half : GQ + HD, :] = (b * cos[...] - a * sin[...]).astype(BF16)
    d_out[GQ + HD :, :] = dv_acc[...].astype(BF16)
    value = dot_nt(normed[...], d_out[...]).astype(BF16)
    quarter = value.shape[0] // 4
    for x in range(2):
        for c in range(2):
            first = (2 * x + c) * quarter
            columns = slice(g_keep.shape[2] - GD, None)
            split_rows(g_keep, g_send, ids[1], x, c, columns, value[first : first + quarter])
    to = 0
    for keep, send in zip(earlier[::2], earlier[1::2]):
        g_keep[:, :, to : to + keep.shape[2]] = keep[...]
        g_send[:, :, to : to + send.shape[2]] = send[...]
        to += keep.shape[2]


def input_kernel(tok, d_mid, w_full, gains, d0, d1, d2, d_tok, d_all):
    width, count = tok.shape
    kv = KVH * HD
    for g, part in enumerate((d0, d1, d2)):
        d_all[g * GQ : (g + 1) * GQ, :] = part[:GQ, :]
        d_all[width + g * HD : width + (g + 1) * HD, :] = part[GQ : GQ + HD, :]
        d_all[width + kv + g * HD : width + kv + (g + 1) * HD, :] = part[GQ + HD :, :]
    gain = gains[:, 0:1]
    for at in range(0, count, BLOCK):
        lanes = slice(at, at + BLOCK)
        x = tok[:, lanes].astype(F32)
        r = lax.rsqrt(jnp.mean(x * x, axis=0, keepdims=True) + EPS)
        z = x * r
        e = dot_nn(w_full[...], d_all[:, lanes]) * gain
        d_tok[:, lanes] = d_mid[:, lanes] + r * (e - z * jnp.mean(e * z, axis=0, keepdims=True))


def row_of(column):
    rows = column.shape[0]
    lanes = (rows + 127) // 128 * 128
    wide = jnp.broadcast_to(column, (rows, 128))
    return jnp.concatenate([wide, jnp.zeros((lanes - rows, 128), F32)], axis=0).T[0, :rows]


def finish_hidden_kernel(
    ids, mine_1, got_1, mine_2, got_2, wg, wu, gains, gate, up, down, g_out, gain_out
):
    shard, core = ids[0], ids[1]
    rows, hidden = wg.shape
    half = rows // 2
    lane = 128
    steps = mine_1.shape[1] // (6 * lane)
    total_steps = hidden // 2 // lane
    sums = []
    for parts, side_of in (((mine_1, mine_2), core), ((got_1, got_2), 1 - core)):
        at = pl.ds(pl.multiple_of(side_of * half, 16), half)
        total = jnp.zeros((half, lane), F32)
        done = (total_steps - steps) * 6 * lane
        g_out[at, :] = parts[1][:, done : done + g_out.shape[1]].astype(F32)
        for turn, turn_steps in enumerate((steps, total_steps - steps)):
            for step in range(turn_steps):
                low = (turn * steps + step) * lane
                begin = step * 6 * lane
                for high in range(2):
                    columns = slice(high * hidden // 2 + low, high * hidden // 2 + low + lane)
                    g = parts[turn][:, begin + high * lane : begin + (high + 1) * lane].astype(F32)
                    u = parts[turn][:, begin + (2 + high) * lane : begin + (3 + high) * lane].astype(F32)
                    gate[at, columns] = g
                    up[at, columns] = u
                    total += wg[at, columns].astype(F32) * g + wu[at, columns].astype(F32) * u
                for side in range(2):
                    d = parts[turn][:, begin + (4 + side) * lane : begin + (5 + side) * lane]
                    to = pl.ds(pl.multiple_of(side_of * rows + side * half, 16), half)
                    down[to, low : low + lane] = d.astype(F32)
        sums.append((at, jnp.sum(total, axis=1, keepdims=True)))
    own = pl.ds(pl.multiple_of(shard * rows, 16), rows)
    gain = gains[own, 1:2]
    first = jnp.where(core == 0, sums[0][1], sums[1][1])
    second = jnp.where(core == 0, sums[1][1], sums[0][1])
    gain_out[...] = row_of(jnp.concatenate([first, second], axis=0) / gain)


def finish_last_kernel(ids, mine, got, wq, wk, wv, gains, g_query, g_key, g_value, gain_out):
    shard, core = ids[0], ids[1]
    rows = wq.shape[0]
    half = rows // 2
    sums = []
    for part, side_of in ((mine, core), (got, 1 - core)):
        at = pl.ds(pl.multiple_of(side_of * half, 16), half)
        total = jnp.zeros((half, 1), F32)
        for weight, grad, begin, length in (
            (wq, g_query, 0, GQ), (wk, g_key, GQ, HD), (wv, g_value, GQ + HD, HD)
        ):
            pieces = [
                part[:, g * GD + begin : g * GD + begin + length] for g in range(KVH)
            ]
            value = jnp.concatenate(pieces, axis=1).astype(F32)
            grad[at, :] = value
            total += jnp.sum(weight[at, :].astype(F32) * value, axis=1, keepdims=True)
        sums.append(total)
    own = pl.ds(pl.multiple_of(shard * rows, 16), rows)
    gain = gains[own, 0:1]
    first = jnp.where(core == 0, sums[0], sums[1])
    second = jnp.where(core == 0, sums[1], sums[0])
    gain_out[...] = row_of(jnp.concatenate([first, second], axis=0) / gain)


SMEM = pl.BlockSpec(memory_space=pltpu.SMEM)


def cost(microseconds):
    return pl.CostEstimate(flops=microseconds * 10**9, bytes_accessed=MIB, transcendentals=0)


def vmem(count):
    return [pl.BlockSpec(memory_space=pltpu.VMEM)] * count


def shape(dims, dtype):
    return jax.ShapeDtypeStruct(dims, dtype)


def after(value, *others):
    return lax.optimization_barrier((value, *others))[0]


class Stages:
    def __init__(self, stages):
        self.stages = stages
        self.now = next(stages)

    def step(self, marker=None):
        if not self.done():
            self.now = self.stages.send(marker)
        return self.marker()

    def done(self):
        return isinstance(self.now, tuple)

    def marker(self):
        return self.now[0] if self.done() else self.now


def shards(
    size, tokens, cotangent, lengths, w_query, w_key, w_value, w_out, attn_gain, w_gate, w_up, w_down,
    mlp_gain,
):
    count, width = tokens.shape
    kv = KVH * HD
    rows = w_query.shape[0]
    quarter = rows // 2
    hidden = w_gate.shape[1]
    part = w_down.shape[0]
    lane = 128
    all_steps = part // lane
    steps = (all_steps * 2 // 3, all_steps - all_steps * 2 // 3)
    chunk = 6 * lane
    rep = lax.axis_index("rep")
    shard = lax.axis_index("shard")
    core = rep % 2
    ids = jnp.stack([shard, core]).astype(jnp.int32)
    bits = size.bit_length() - 1

    def over_x(value):
        return lax.ppermute(value, "shard", [(0, 1), (1, 0)])

    def over_rep(value, bit):
        return lax.ppermute(value, "rep", [(i, i ^ (1 << bit)) for i in range(size)])

    def pick(value, axis, index, total):
        step = value.shape[axis] // total
        return lax.dynamic_slice_in_dim(value, index * step, step, axis)

    tok = tokens.T
    cot = cotangent.T
    down = w_down.T
    params = pltpu.CompilerParams(vmem_limit_bytes=56 * MIB)
    packed = pl.pallas_call(
        pack_first_kernel,
        out_shape=shape((quarter + 16, width + 2 * kv), BF16),
        in_specs=[SMEM] + vmem(5),
        out_specs=pl.BlockSpec(memory_space=pltpu.VMEM),
        cost_estimate=cost(2),
        name="pack_first",
    )(ids, w_query, w_key, w_value, attn_gain, mlp_gain)
    second, third = pl.pallas_call(
        pack_rest_kernel,
        out_shape=(
            shape((quarter, (steps[0] + 1) * chunk), BF16),
            shape((quarter, steps[1] * chunk), BF16),
        ),
        in_specs=[SMEM] + vmem(4),
        out_specs=vmem(2),
        compiler_params=params,
        cost_estimate=cost(3),
        name="pack_rest",
    )(after(ids, packed), w_gate, w_up, down, w_out)
    ends = jnp.cumsum(lengths[0], dtype=jnp.int32)
    begins = ends - lengths[0]
    row_ids = jnp.arange(count, dtype=jnp.int32)
    starts = jnp.max(jnp.where(row_ids[None, :] >= begins[:, None], begins[:, None], 0), axis=0)
    offset = (row_ids - starts).astype(F32)
    frequency = THETA ** (-2.0 * jnp.arange(HD // 2, dtype=F32) / HD)
    angles = frequency[:, None] * offset[None, :]
    cos = jnp.cos(angles)
    sin = jnp.sin(angles)
    at = jnp.arange(count // BLOCK, dtype=jnp.int32)
    first = jnp.max(jnp.where(at[:, None] * BLOCK >= begins[None, :], begins[None, :], 0), axis=1)
    need = (at + 1) * (BLOCK // STRIP) - first // STRIP
    starts = starts[None, :]

    first_a = after(over_x(packed), second, cos, sin, starts, need)
    first_b = over_rep(first_a, 0)
    second = after(second, first_a)

    w_full, gains, normed, q, k, v = pl.pallas_call(
        project_kernel,
        out_shape=(
            shape((width, width + 2 * kv), BF16),
            shape((width, 8), F32),
            shape((width, count), BF16),
            shape((width, count), BF16),
            shape((kv, count), BF16),
            shape((kv, count), BF16),
        ),
        in_specs=[SMEM] + vmem(9),
        out_specs=vmem(6),
        compiler_params=params,
        cost_estimate=cost(5),
        name="project",
    )(after(ids, second), tok, w_query, w_key, w_value, packed, first_a, first_b, cos, sin)

    def one(size_of, index):
        return pl.BlockSpec((size_of, count), lambda i: (index, 0))

    atts, lows, lses = [], [], []
    for g in range(KVH):
        att, low, lse = pl.pallas_call(
            attend_kernel,
            grid=(1,),
            out_shape=(shape((GQ, count), F32), shape((GQ, count), BF16), shape((8, count), F32)),
            in_specs=[SMEM, one(1, 0), one(GQ, g), one(HD, g), one(HD, g)],
            out_specs=(one(GQ, 0), one(GQ, 0), one(8, 0)),
            compiler_params=params,
            cost_estimate=cost(7),
            name="attend",
        )(after(need, *lses[-1:]), starts, q, k, v)
        atts.append(att)
        lows.append(low)
        lses.append(lse)

    second_a = after(over_x(second), lses[-1])
    third = after(third, second_a)
    second_b = over_rep(second_a, 0)

    def whole(dims):
        return pl.BlockSpec(dims, lambda i: (0,) * len(dims))

    def hidden_specs(turn):
        begin = turn * steps[0]
        low = pl.BlockSpec((rows, lane), lambda i: (0, begin + i))
        high = pl.BlockSpec((rows, lane), lambda i: (0, all_steps + begin + i))
        return [
            low, high, low, high,
            pl.BlockSpec((width, lane), lambda i: (0, begin + i)),
            pl.BlockSpec((quarter, chunk), lambda i: (0, i)),
            pl.BlockSpec((quarter, chunk), lambda i: (0, i)),
        ]

    wide = whole((width, count))
    anywhere = pl.BlockSpec(memory_space=pl.ANY)
    att_specs = [whole((GQ, count))] * KVH
    grad_spec = pl.BlockSpec((2, quarter, chunk), lambda i: (0, 0, i))
    grad_shapes = [
        shape((2, quarter, chunk * steps[0]), BF16),
        shape((2, quarter, chunk * (steps[1] + 1)), BF16),
    ]
    weight_scratch = [pltpu.VMEM((width, 2 * lane), BF16)] * 3 + [pltpu.VMEM((count, width), BF16)] * 2
    wo_spec = pl.BlockSpec((quarter, chunk), lambda i: (0, steps[0]))
    mid, nm, acc_out, acc_e, wo, keep_1, send_1 = pl.pallas_call(
        middle_first_kernel,
        grid=(steps[0],),
        out_shape=(
            shape((width, count), F32),
            shape((width, count), BF16),
            shape((width, count), F32),
            shape((width, count), F32),
            shape((width, width), BF16),
            grad_shapes[0],
            grad_shapes[0],
        ),
        in_specs=[SMEM, wide, wide] + att_specs
        + [whole((width, 8)), whole((rows, width)), wo_spec, wo_spec] + hidden_specs(0),
        out_specs=(anywhere, anywhere, wide, wide, anywhere, grad_spec, grad_spec),
        scratch_shapes=weight_scratch
        + [
            pltpu.VMEM((width, count), F32),
            pltpu.VMEM((width, count), BF16),
            pltpu.VMEM((width, width), BF16),
            pltpu.SemaphoreType.DMA((3,)),
        ],
        compiler_params=params,
        cost_estimate=cost(18),
        name="middle_first",
    )(
        after(ids, third), tok, cot, *lows, gains, w_out, second_a, second_b,
        w_gate, w_gate, w_up, w_up, down, second_a, second_b,
    )

    def scatter_x(total):
        return pick(total, 0, shard, 2)[0], pick(total, 0, 1 - shard, 2)[0]

    def half_of(total, bit, axis):
        side = (rep >> bit) % 2
        return pick(total, axis, side, 2), pick(total, axis, 1 - side, 2)

    def join(total, got, bit, axis):
        side = (rep >> bit) % 2
        return jnp.where(
            side == 0,
            jnp.concatenate([total, got], axis=axis),
            jnp.concatenate([got, total], axis=axis),
        )

    def reduce_steps(keep, send, cuts):
        def end(value, marker):
            return value if marker is None else after(value, marker)

        sent = send
        marker = yield sent
        total = keep + end(over_rep(sent, 0), marker)
        stay, sent = scatter_x(total)
        marker = yield sent
        total = stay + end(over_x(sent), marker)
        done = []
        for bit in range(1, bits):
            if bit in cuts:
                stay, sent = half_of(total, bit, cuts[bit])
                done.append(bit)
            else:
                stay = sent = total
            marker = yield sent
            total = stay + end(over_rep(sent, bit), marker)
        for bit in reversed(done):
            marker = yield total
            total = join(total, end(over_rep(total, bit), marker), bit, cuts[bit])
        marker = yield total
        yield total, end(over_rep(total, 0), marker)

    third_a = after(over_x(third), mid)
    third_b = over_rep(third_a, 0)
    run_1 = Stages(reduce_steps(keep_1, after(send_1, third_a), {1: 0, 2: 1}))
    out, d_mid, d_att, keep_2, send_2 = pl.pallas_call(
        middle_second_kernel,
        grid=(steps[1],),
        out_shape=(
            shape((width, count), BF16),
            shape((width, count), F32),
            shape((width, count), BF16),
            grad_shapes[1],
            grad_shapes[1],
        ),
        in_specs=[SMEM, wide, wide, whole((width, 8))] + [anywhere] * (KVH + 4) + hidden_specs(1),
        out_specs=(
            anywhere, anywhere, anywhere, whole(grad_shapes[1].shape), whole(grad_shapes[1].shape),
        ),
        scratch_shapes=weight_scratch
        + [pltpu.VMEM((width, count), F32)] * 2
        + [pltpu.VMEM((width, count), BF16), pltpu.VMEM((width, width), BF16)]
        + [pltpu.VMEM((width, count), F32)] * 3
        + [pltpu.VMEM((width, count), BF16)] * 2
        + [pltpu.SemaphoreType.DMA((10,))],
        compiler_params=params,
        cost_estimate=cost(18),
        name="middle_second",
    )(
        after(ids, run_1.step()), cot, nm, gains, *lows, wo, mid, acc_out, acc_e,
        w_gate, w_gate, w_up, w_up, down, third_a, third_b,
    )
    run_2 = Stages(reduce_steps(keep_2, send_2, {1: 0, 2: 1}))
    sent = [run_1.step(d_mid), run_2.step()]

    d_parts, earlier = [], []
    for g in range(KVH):
        joined = earlier if g == KVH - 1 else []
        grads_to = (2, quarter, GD + sum(x.shape[2] for x in joined[::2]))
        d_part, *pair = pl.pallas_call(
            attend_back_kernel,
            grid=(1,),
            out_shape=(
                shape((GD, count), BF16),
                shape(grads_to, BF16),
                shape(grads_to, BF16),
            ),
            in_specs=[
                SMEM, SMEM, one(1, 0), one(GQ, g), one(HD, g), one(HD, g), one(GQ, g), one(GQ, 0),
                one(8, 0), one(HD // 2, 0), one(HD // 2, 0), one(width, 0),
            ] + [whole(x.shape) for x in joined],
            out_specs=(one(GD, 0), whole(grads_to), whole(grads_to)),
            scratch_shapes=[pltpu.VMEM((HD, count), F32), pltpu.VMEM((HD, count), F32)],
            compiler_params=params,
            cost_estimate=cost(10),
            name="attend_back",
        )(
            after(ids, *sent), need, starts, q, k, v, d_att, atts[g], lses[g],
            cos, sin, normed, *joined,
        )
        d_parts.append(d_part)
        earlier += pair
        sent = [run_1.step(d_part), run_2.step(d_part)]
    run_3 = Stages(reduce_steps(pair[0], after(pair[1], *sent), {1: 0}))
    sent.append(run_3.step())

    d_tok = pl.pallas_call(
        input_kernel,
        out_shape=shape((width, count), F32),
        in_specs=vmem(7),
        out_specs=pl.BlockSpec(memory_space=pltpu.VMEM),
        scratch_shapes=[pltpu.VMEM((width + 2 * kv, count), BF16)],
        compiler_params=params,
        cost_estimate=cost(7),
        name="input_grad",
    )(after(tok, *sent), d_mid, w_full, gains, *d_parts)

    sent = run_3.step(d_tok)
    run_1.step(after(d_tok, sent))
    run_2.step(after(d_tok, sent))
    sent = run_3.step()
    run_1.step(sent)
    run_2.step(sent)
    sent = run_3.step()
    run_1.step(sent)
    sent = run_3.step()
    while not (run_1.done() and run_2.done()):
        run_1.step(sent)
        run_2.step(sent)
    gain_shape = shape((rows,), F32)
    grad_gate, grad_up, grad_down, grad_out, grad_mlp_gain = pl.pallas_call(
        finish_hidden_kernel,
        out_shape=(
            shape((rows, hidden), F32), shape((rows, hidden), F32), shape((width, part), F32),
            shape((rows, width), F32), gain_shape,
        ),
        in_specs=[SMEM] + vmem(7),
        out_specs=vmem(5),
        compiler_params=params,
        cost_estimate=cost(5),
        name="finish_hidden",
    )(after(ids, sent), *run_1.now, *run_2.now, w_gate, w_up, gains)
    run_3.step(grad_mlp_gain)
    while not run_3.done():
        run_3.step()
    grad_query, grad_key, grad_value, grad_attn_gain = pl.pallas_call(
        finish_last_kernel,
        out_shape=(
            shape((rows, width), F32), shape((rows, kv), F32), shape((rows, kv), F32), gain_shape
        ),
        in_specs=[SMEM] + vmem(6),
        out_specs=vmem(4),
        compiler_params=params,
        cost_estimate=cost(3),
        name="finish_last",
    )(ids, *run_3.now, w_query, w_key, w_value, gains)
    grad_down = grad_down.T
    return (
        out.T, d_tok.T, grad_query, grad_key, grad_value, grad_out, grad_attn_gain,
        grad_gate, grad_up, grad_down, grad_mlp_gain,
    )


def solution(mesh):
    everywhere = P(("rep", "shard"), None)
    weight = P("shard", None)
    gain = P("shard")
    return jax.shard_map(
        functools.partial(shards, mesh.shape["rep"]),
        mesh=mesh,
        in_specs=(
            everywhere, everywhere, everywhere, weight, weight, weight, weight, gain, weight, weight,
            weight, gain,
        ),
        out_specs=(
            everywhere, everywhere, weight, weight, weight, weight, gain, weight, weight, weight, gain,
        ),
        check_vma=False,
    )
```

```python
import functools

import jax
import jax.numpy as jnp
from jax import lax
from jax.experimental import pallas as pl
from jax.experimental.pallas import tpu as pltpu
from jax.sharding import PartitionSpec as P

H = 9
KVH = 3
HD = 64
MAXLEN = 512
EPS = 1e-05
THETA = 100000.0
BLOCK = 256
STRIP = 128
GROUPS = H // KVH
GQ = GROUPS * HD
GD = GQ + 2 * HD
SCALE = HD ** (-0.5)
F32 = jnp.float32
BF16 = jnp.bfloat16
MIB = 1024 * 1024


def dot_nn(left, right):
    return lax.dot_general(left, right, (((1,), (0,)), ((), ())), preferred_element_type=F32)


def dot_nt(left, right):
    return lax.dot_general(left, right, (((1,), (1,)), ((), ())), preferred_element_type=F32)


def dot_tn(left, right):
    return lax.dot_general(left, right, (((0,), (0,)), ((), ())), preferred_element_type=F32)


def put_rows(full, own, got_a, got_b, shard, core):
    rows = own.shape[0]
    half = rows // 2
    full[pl.ds(pl.multiple_of(shard * rows, 16), rows), :] = own[...]
    other = (1 - shard) * rows
    full[pl.ds(pl.multiple_of(other + core * half, 16), half), :] = got_a[...]
    full[pl.ds(pl.multiple_of(other + (1 - core) * half, 16), half), :] = got_b[...]


def pack_first_kernel(wq, wk, wv, attn_gain, mlp_gain, packed):
    core = lax.axis_index("rep") % 2
    rows, width = wq.shape
    part = rows // 2
    half = pl.ds(pl.multiple_of(core * part, 16), part)
    packed[:part, :width] = wq[half, :]
    packed[:part, width : width + KVH * HD] = wk[half, :]
    packed[:part, width + KVH * HD :] = wv[half, :]
    row = lax.broadcasted_iota(jnp.int32, (packed.shape[0] - part, rows), 0)
    first = attn_gain[...].astype(F32).reshape(1, rows)
    second = mlp_gain[...].astype(F32).reshape(1, rows)
    packed[part:, :rows] = jnp.where(row == 0, first, jnp.where(row == 1, second, 0.0)).astype(BF16)


def pack_rest_kernel(ids, wg, wu, wd, wo, packed_0, packed_1):
    core = ids[1]
    rows = wg.shape[0]
    part = rows // 2
    lane = 128
    shift = wg.shape[1] // 2
    steps = packed_1.shape[1] // (6 * lane)
    first = shift // lane - steps
    half = pl.ds(pl.multiple_of(core * part, 16), part)
    for packed, begin, end in ((packed_0, 0, first), (packed_1, first, first + steps)):
        for step in range(begin, end):
            low = slice(step * lane, (step + 1) * lane)
            high = slice(shift + low.start, shift + low.stop)
            to = (step - begin) * 6 * lane
            for at, (source, columns) in enumerate(((wg, low), (wg, high), (wu, low), (wu, high))):
                packed[:, to + at * lane : to + (at + 1) * lane] = source[half, columns]
            for side in range(2):
                down = pl.ds(pl.multiple_of(core * rows + side * part, 16), part)
                packed[:, to + (4 + side) * lane : to + (5 + side) * lane] = wd[down, low]
    to = first * 6 * lane
    packed_0[:, to : to + wo.shape[1]] = wo[half, :]


def project_kernel(
    ids, tok, wq, wk, wv, packed, got_a, got_b, cos, sin,
    w_full, gains, normed, q_out, k_out, v_out,
):
    shard, core = ids[0], ids[1]
    rows = wq.shape[0]
    own = pl.ds(pl.multiple_of(shard * rows, 16), rows)
    part = rows // 2
    other = (1 - shard) * rows
    w_full[own, : wq.shape[1]] = wq[...]
    w_full[own, wq.shape[1] : wq.shape[1] + KVH * HD] = wk[...]
    w_full[own, wq.shape[1] + KVH * HD :] = wv[...]
    w_full[pl.ds(pl.multiple_of(other + core * part, 16), part), :] = got_a[:part, :]
    w_full[pl.ds(pl.multiple_of(other + (1 - core) * part, 16), part), :] = got_b[:part, :]
    lanes = (rows + 127) // 128 * 128
    gains[own, :] = packed[part:, :lanes].astype(F32).T[:rows, :8]
    gains[pl.ds(pl.multiple_of(other, 16), rows), :] = got_a[part:, :lanes].astype(F32).T[:rows, :8]
    width, count = tok.shape
    kv = KVH * HD
    half = HD // 2
    gain = gains[:, 0:1]
    for at in range(0, count, BLOCK):
        lanes = slice(at, at + BLOCK)
        x = tok[:, lanes].astype(F32)
        r = lax.rsqrt(jnp.mean(x * x, axis=0, keepdims=True) + EPS)
        normed[:, lanes] = (x * r * gain).astype(BF16)
    for at in range(0, count, BLOCK):
        lanes = slice(at, at + BLOCK)
        pre = dot_tn(w_full[...], normed[:, lanes])
        c = cos[:, lanes]
        s = sin[:, lanes]
        for head in range(H + KVH):
            row = head * HD
            a = pre[row : row + half]
            b = pre[row + half : row + HD]
            front = a * c - b * s
            back = b * c + a * s
            if head < H:
                q_out[row : row + half, lanes] = (front * SCALE).astype(BF16)
                q_out[row + half : row + HD, lanes] = (back * SCALE).astype(BF16)
            else:
                row -= width
                k_out[row : row + half, lanes] = front.astype(BF16)
                k_out[row + half : row + HD, lanes] = back.astype(BF16)
        v_out[:, lanes] = pre[width + kv :].astype(BF16)


def side_by_side(ref, lanes, rows=HD):
    return jnp.concatenate([ref[j * rows : (j + 1) * rows, lanes] for j in range(GROUPS)], axis=1)


def span_of(at, strips):
    return pl.ds(pl.multiple_of((at + 1) * BLOCK - strips * STRIP, STRIP), strips * STRIP)


def window(at, strips, starts):
    rows = lax.broadcasted_iota(jnp.int32, (strips * STRIP, GROUPS * BLOCK), 0)
    rows += span_of(at, strips).start
    columns = at * BLOCK + lax.broadcasted_iota(jnp.int32, (1, BLOCK), 1)
    starts = jnp.concatenate([starts] * GROUPS, axis=1)
    columns = jnp.concatenate([columns] * GROUPS, axis=1)
    return (rows >= starts) & (rows <= columns)


def reaches(count):
    own = BLOCK // STRIP
    return range(own, min(count // STRIP, own + (MAXLEN + STRIP - 2) // STRIP) + 1)


def attend_kernel(need, starts, q, k, v, att, att_low, lse, k_rows):
    count = q.shape[1]
    k_rows[...] = k[...].T

    @pl.loop(0, count // BLOCK)
    def _(at):
        lanes = pl.ds(pl.multiple_of(at * BLOCK, BLOCK), BLOCK)
        for strips in reaches(count):

            @pl.when(need[at] == strips)
            def _(strips=strips):
                ok = window(at, strips, starts[:, lanes])
                span = span_of(at, strips)
                scores = jnp.where(ok, dot_nn(k_rows[span, :], side_by_side(q, lanes)), -1e30)
                top = jnp.max(scores, axis=0, keepdims=True)
                e = jnp.exp(scores - top)
                total = jnp.sum(e, axis=0, keepdims=True)
                o = dot_nn(v[:, span], e.astype(BF16)) / total
                logs = top + jnp.log(total)
                for j in range(GROUPS):
                    rows = slice(j * HD, (j + 1) * HD)
                    one = slice(j * BLOCK, (j + 1) * BLOCK)
                    att[rows, lanes] = o[:, one]
                    att_low[rows, lanes] = o[:, one].astype(BF16)
                    lse[j : j + 1, lanes] = logs[:, one]


def place(target, shard, core, x, c, columns, value):
    away = jnp.where(core == c, 0, 2) + jnp.where(shard == x, 0, 1)
    target[away, :, columns] = value


def hidden_step(
    ids, cot, cot_rows, nm, nm_rows, acc_out, acc_e,
    wg_lo, wg_hi, wu_lo, wu_hi, wd_own, got_a, got_b, grads, wg, wu, wd, base,
):
    shard, core = ids[0], ids[1]
    width = cot.shape[0]
    rows, lane = wg_lo.shape
    half = rows // 2
    own = pl.ds(pl.multiple_of(shard * rows, 16), rows)
    other = (1 - shard) * rows
    at_a = pl.ds(pl.multiple_of(other + core * half, 16), half)
    at_b = pl.ds(pl.multiple_of(other + (1 - core) * half, 16), half)
    wg[own, :lane] = wg_lo[...]
    wg[own, lane:] = wg_hi[...]
    wu[own, :lane] = wu_lo[...]
    wu[own, lane:] = wu_hi[...]
    for at, got in ((at_a, got_a), (at_b, got_b)):
        wg[at, :] = got[:, : 2 * lane]
        wu[at, :] = got[:, 2 * lane : 4 * lane]
    for turn in range(2):

        @pl.when(shard == turn)
        def _(turn=turn):
            wd[:, turn * lane : (turn + 1) * lane] = wd_own[...]
            columns = slice((1 - turn) * lane, (2 - turn) * lane)
            for side in range(2):
                from_a = pl.ds(pl.multiple_of(core * rows + side * half, 16), half)
                from_b = pl.ds(pl.multiple_of((1 - core) * rows + side * half, 16), half)
                source = slice((4 + side) * lane, (5 + side) * lane)
                wd[from_a, columns] = got_a[:, source]
                wd[from_b, columns] = got_b[:, source]

    gate = dot_nn(nm_rows[...], wg[...])
    up = dot_nn(nm_rows[...], wu[...])
    dh = dot_nn(cot_rows[...], wd[...])
    sg = jax.nn.sigmoid(gate)
    sw = gate * sg
    hid = (sw * up).astype(BF16)
    dg = (dh * up * sg * (1.0 + gate * (1.0 - sg))).astype(BF16)
    du = (dh * sw).astype(BF16)
    acc_out[...] += dot_nt(wd[...], hid)
    acc_e[...] += dot_nt(wg[...], dg) + dot_nt(wu[...], du)
    g_gate = dot_nn(nm[...], dg).astype(BF16)
    g_up = dot_nn(nm[...], du).astype(BF16)
    g_down = dot_nn(cot[...], hid).astype(BF16)
    for x in range(2):
        for c in range(2):
            first = (2 * x + c) * half
            at_gate = pl.ds(pl.multiple_of(base, lane), 2 * lane)
            at_up = pl.ds(pl.multiple_of(base + 2 * lane, lane), 2 * lane)
            place(grads, shard, core, x, c, at_gate, g_gate[first : first + half])
            place(grads, shard, core, x, c, at_up, g_up[first : first + half])
            for side in range(2):
                first = c * rows + side * half
                value = g_down[first : first + half, x * lane : (x + 1) * lane]
                columns = pl.ds(pl.multiple_of(base + (4 + side) * lane, lane), lane)
                place(grads, shard, core, x, c, columns, value)


def middle_first_kernel(
    ids, tok, cot, att0, att1, att2, gains, wo_own, wo_a, wo_b,
    wg_lo, wg_hi, wu_lo, wu_hi, wd_own, got_a, got_b,
    mid_out, nm_out, acc_out, acc_e, wo_out, grads_0, grads_1, grads_2, grads_3,
    wg, wu, wd, nm_rows, cot_rows, mid, nm, wo, grads, sems, grad_sems,
):
    step = pl.program_id(0)
    block = 6 * wg_lo.shape[1]
    columns = pl.ds(pl.multiple_of(step * block, 128), block)
    outs = (grads_0, grads_1, grads_2, grads_3)
    leave = [
        pltpu.make_async_copy(grads.at[at, :, columns], out.at[:, columns], grad_sems.at[at])
        for at, out in enumerate(outs)
    ]
    copies = [
        pltpu.make_async_copy(source, target, sems.at[at])
        for at, (source, target) in enumerate(((mid, mid_out), (nm, nm_out), (wo, wo_out)))
    ]

    @pl.when(step == 0)
    def _():
        width = wo.shape[0]
        put_rows(wo, wo_own, wo_a.at[:, :width], wo_b.at[:, :width], ids[0], ids[1])
        copies[2].start()
        gain = gains[:, 1:2]
        att = jnp.concatenate([att0[...], att1[...], att2[...]], axis=0)
        mid[...] = tok[...].astype(F32) + dot_tn(wo[...], att)
        copies[0].start()
        for at in range(0, tok.shape[1], BLOCK):
            lanes = slice(at, at + BLOCK)
            m = mid[:, lanes]
            r = lax.rsqrt(jnp.mean(m * m, axis=0, keepdims=True) + EPS)
            part = (m * r * gain).astype(BF16)
            nm[:, lanes] = part
            nm_rows[lanes, :] = part.T
            cot_rows[lanes, :] = cot[:, lanes].T
        copies[1].start()
        acc_out[...] = jnp.zeros_like(acc_out)
        acc_e[...] = jnp.zeros_like(acc_e)

    hidden_step(
        ids, cot, cot_rows, nm, nm_rows, acc_out, acc_e,
        wg_lo, wg_hi, wu_lo, wu_hi, wd_own, got_a, got_b, grads, wg, wu, wd, step * block,
    )

    for copy in leave:
        copy.start()

    @pl.when(step == pl.num_programs(0) - 1)
    def _():
        for copy in copies:
            copy.wait()
        for at, out in enumerate(outs):
            pltpu.make_async_copy(grads.at[at], out, grad_sems.at[at]).wait()


def middle_second_kernel(
    ids, cot, nm, gains, att0, att1, att2, wo_in, mid_in, out_in, e_in,
    wg_lo, wg_hi, wu_lo, wu_hi, wd_own, got_a, got_b,
    out_out, d_mid_out, d_att_out, grads_0, grads_1, grads_2, grads_3,
    wg, wu, wd, nm_rows, cot_rows, acc_out, acc_e, att, wo, mid, out_first, e_first, out, d_att, grads,
    sems, grad_sems,
):
    step = pl.program_id(0)
    rows = att0.shape[0]
    arrive = [
        (att0, att.at[:rows, :]), (att1, att.at[rows : 2 * rows, :]), (att2, att.at[2 * rows :, :]),
        (wo_in, wo), (mid_in, mid), (out_in, out_first), (e_in, e_first),
    ]
    arrive = [pltpu.make_async_copy(*pair, sems.at[at]) for at, pair in enumerate(arrive)]
    leave = [(out, out_out), (mid, d_mid_out), (d_att, d_att_out)]
    leave = [pltpu.make_async_copy(*pair, sems.at[7 + at]) for at, pair in enumerate(leave)]
    grads_leave = [
        pltpu.make_async_copy(grads.at[at], out_at, grad_sems.at[at])
        for at, out_at in enumerate((grads_0, grads_1, grads_2, grads_3))
    ]

    @pl.when(step == 0)
    def _():
        for copy in arrive:
            copy.start()
        for at in range(0, cot.shape[1], BLOCK):
            lanes = slice(at, at + BLOCK)
            nm_rows[lanes, :] = nm[:, lanes].T
            cot_rows[lanes, :] = cot[:, lanes].T
        acc_out[...] = jnp.zeros_like(acc_out)
        acc_e[...] = jnp.zeros_like(acc_e)

    hidden_step(
        ids, cot, cot_rows, nm, nm_rows, acc_out, acc_e,
        wg_lo, wg_hi, wu_lo, wu_hi, wd_own, got_a, got_b, grads, wg, wu, wd,
        step * (6 * wg_lo.shape[1]),
    )

    @pl.when(step == pl.num_programs(0) - 1)
    def _():
        for copy in arrive:
            copy.wait()
        out[...] = (mid[...] + out_first[...] + acc_out[...]).astype(BF16)
        leave[0].start()
        gain = gains[:, 1:2]
        for at in range(0, cot.shape[1], BLOCK):
            lanes = slice(at, at + BLOCK)
            m = mid[:, lanes]
            r = lax.rsqrt(jnp.mean(m * m, axis=0, keepdims=True) + EPS)
            z = m * r
            e = (e_first[:, lanes] + acc_e[:, lanes]) * gain
            d_part = cot[:, lanes].astype(F32) + r * (e - z * jnp.mean(e * z, axis=0, keepdims=True))
            mid[:, lanes] = d_part
            nm_rows[lanes, :] = d_part.astype(BF16).T
        leave[1].start()
        low = nm_rows[...]
        d_att[...] = dot_nt(wo[...], low).astype(BF16)
        leave[2].start()
        value = dot_nn(att[...], low).astype(BF16)
        half = value.shape[0] // 4
        done = pl.num_programs(0) * 6 * wg_lo.shape[1]
        for x in range(2):
            for c in range(2):
                first = (2 * x + c) * half
                columns = slice(done, done + value.shape[1])
                place(grads, ids[0], ids[1], x, c, columns, value[first : first + half])
        for copy in grads_leave:
            copy.start()
        for copy in leave + grads_leave:
            copy.wait()


def attend_back_kernel(ids, need, starts, q, k, v, d_att, att, lse, cos, sin, normed, *refs):
    *refs, dk_acc, dv_acc, k_rows, v_rows = refs
    earlier = refs[:2] if len(refs) > 2 else []
    d_out, *targets = refs[len(earlier) :]
    count = q.shape[1]
    half = HD // 2
    k_rows[...] = k[...].T
    v_rows[...] = v[...].T
    dk_acc[...] = jnp.zeros_like(dk_acc)
    dv_acc[...] = jnp.zeros_like(dv_acc)

    @pl.loop(0, count // BLOCK)
    def _(at):
        lanes = pl.ds(pl.multiple_of(at * BLOCK, BLOCK), BLOCK)
        for strips in reaches(count):

            @pl.when(need[at] == strips)
            def _(strips=strips):
                ok = window(at, strips, starts[:, lanes])
                span = span_of(at, strips)
                c = cos[:, lanes]
                s = sin[:, lanes]
                q_part = side_by_side(q, lanes)
                d_part = side_by_side(d_att, lanes)
                scores = jnp.where(ok, dot_nn(k_rows[span, :], q_part), -1e30)
                probs = jnp.exp(scores - side_by_side(lse, lanes, 1))
                d_probs = dot_nn(v_rows[span, :], d_part)
                centre = jnp.sum(
                    d_part.astype(F32) * side_by_side(att, lanes), axis=0, keepdims=True
                )
                d_scores = (probs * (d_probs - centre)).astype(BF16)
                dq = dot_nn(k[:, span], d_scores) * SCALE
                for j in range(GROUPS):
                    one = slice(j * BLOCK, (j + 1) * BLOCK)
                    a = dq[:half, one]
                    b = dq[half:, one]
                    d_out[j * HD : j * HD + half, lanes] = (a * c + b * s).astype(BF16)
                    d_out[j * HD + half : (j + 1) * HD, lanes] = (b * c - a * s).astype(BF16)
                dk_acc[:, span] += dot_nt(q_part, d_scores)
                dv_acc[:, span] += dot_nt(d_part, probs.astype(BF16))
    a = dk_acc[:half, :]
    b = dk_acc[half:, :]
    d_out[GQ : GQ + half, :] = (a * cos[...] + b * sin[...]).astype(BF16)
    d_out[GQ + half : GQ + HD, :] = (b * cos[...] - a * sin[...]).astype(BF16)
    d_out[GQ + HD :, :] = dv_acc[...].astype(BF16)
    value = dot_nt(normed[...], d_out[...]).astype(BF16)
    quarter = value.shape[0] // 4
    for x in range(2):
        for c in range(2):
            first = (2 * x + c) * quarter
            part = value[first : first + quarter]
            if not earlier:
                place(targets[0], ids[0], ids[1], x, c, slice(None), part)
            for away, target in enumerate(targets if earlier else []):

                @pl.when((away // 2 == (ids[1] ^ c)) & (away % 2 == (ids[0] ^ x)))
                def _(target=target, part=part):
                    target[:, len(earlier) * GD :] = part

    for at, group in enumerate(earlier):
        for away, target in enumerate(targets):
            target[:, at * GD : (at + 1) * GD] = group[away]


def input_kernel(tok, d_mid, w_full, gains, d0, d1, d2, d_tok, d_all):
    width, count = tok.shape
    kv = KVH * HD
    for g, part in enumerate((d0, d1, d2)):
        d_all[g * GQ : (g + 1) * GQ, :] = part[:GQ, :]
        d_all[width + g * HD : width + (g + 1) * HD, :] = part[GQ : GQ + HD, :]
        d_all[width + kv + g * HD : width + kv + (g + 1) * HD, :] = part[GQ + HD :, :]
    gain = gains[:, 0:1]
    for at in range(0, count, BLOCK):
        lanes = slice(at, at + BLOCK)
        x = tok[:, lanes].astype(F32)
        r = lax.rsqrt(jnp.mean(x * x, axis=0, keepdims=True) + EPS)
        z = x * r
        e = dot_nn(w_full[...], d_all[:, lanes]) * gain
        d_tok[:, lanes] = d_mid[:, lanes] + r * (e - z * jnp.mean(e * z, axis=0, keepdims=True))


def row_of(column):
    rows = column.shape[0]
    lanes = (rows + 127) // 128 * 128
    wide = jnp.broadcast_to(column, (rows, 128))
    return jnp.concatenate([wide, jnp.zeros((lanes - rows, 128), F32)], axis=0).T[0, :rows]


def finish_hidden_kernel(
    ids, mine_1, got_1, mine_2, got_2, wg, wu, gains, gate, up, down, g_out, gain_out
):
    shard, core = ids[0], ids[1]
    rows, hidden = wg.shape
    half = rows // 2
    lane = 128
    steps = mine_1.shape[1] // (6 * lane)
    total_steps = hidden // 2 // lane
    sums = []
    for parts, side_of in (((mine_1, mine_2), core), ((got_1, got_2), 1 - core)):
        at = pl.ds(pl.multiple_of(side_of * half, 16), half)
        total = jnp.zeros((half, lane), F32)
        done = (total_steps - steps) * 6 * lane
        g_out[at, :] = parts[1][:, done : done + g_out.shape[1]].astype(F32)
        for turn, turn_steps in enumerate((steps, total_steps - steps)):
            for step in range(turn_steps):
                low = (turn * steps + step) * lane
                begin = step * 6 * lane
                for high in range(2):
                    columns = slice(high * hidden // 2 + low, high * hidden // 2 + low + lane)
                    g = parts[turn][:, begin + high * lane : begin + (high + 1) * lane].astype(F32)
                    u = parts[turn][:, begin + (2 + high) * lane : begin + (3 + high) * lane].astype(F32)
                    gate[at, columns] = g
                    up[at, columns] = u
                    total += wg[at, columns].astype(F32) * g + wu[at, columns].astype(F32) * u
                for side in range(2):
                    d = parts[turn][:, begin + (4 + side) * lane : begin + (5 + side) * lane]
                    to = pl.ds(pl.multiple_of(side_of * rows + side * half, 16), half)
                    down[to, low : low + lane] = d.astype(F32)
        sums.append((at, jnp.sum(total, axis=1, keepdims=True)))
    own = pl.ds(pl.multiple_of(shard * rows, 16), rows)
    gain = gains[own, 1:2]
    first = jnp.where(core == 0, sums[0][1], sums[1][1])
    second = jnp.where(core == 0, sums[1][1], sums[0][1])
    gain_out[...] = row_of(jnp.concatenate([first, second], axis=0) / gain)


def finish_last_kernel(ids, mine, got, wq, wk, wv, gains, g_query, g_key, g_value, gain_out):
    shard, core = ids[0], ids[1]
    rows = wq.shape[0]
    half = rows // 2
    sums = []
    for part, side_of in ((mine, core), (got, 1 - core)):
        at = pl.ds(pl.multiple_of(side_of * half, 16), half)
        total = jnp.zeros((half, 1), F32)
        for weight, grad, begin, length in (
            (wq, g_query, 0, GQ), (wk, g_key, GQ, HD), (wv, g_value, GQ + HD, HD)
        ):
            pieces = [
                part[:, g * GD + begin : g * GD + begin + length] for g in range(KVH)
            ]
            value = jnp.concatenate(pieces, axis=1).astype(F32)
            grad[at, :] = value
            total += jnp.sum(weight[at, :].astype(F32) * value, axis=1, keepdims=True)
        sums.append(total)
    own = pl.ds(pl.multiple_of(shard * rows, 16), rows)
    gain = gains[own, 0:1]
    first = jnp.where(core == 0, sums[0], sums[1])
    second = jnp.where(core == 0, sums[1], sums[0])
    gain_out[...] = row_of(jnp.concatenate([first, second], axis=0) / gain)


SMEM = pl.BlockSpec(memory_space=pltpu.SMEM)


def cost(microseconds):
    return pl.CostEstimate(flops=microseconds * 10**9, bytes_accessed=MIB, transcendentals=0)


def vmem(count):
    return [pl.BlockSpec(memory_space=pltpu.VMEM)] * count


def shape(dims, dtype):
    return jax.ShapeDtypeStruct(dims, dtype)


def after(value, *others):
    return lax.optimization_barrier((value, *others))[0]


class Stages:
    def __init__(self, stages):
        self.stages = stages
        self.now = next(stages)

    def step(self, marker=None):
        if not self.done():
            self.now = self.stages.send(marker)
        return self.marker()

    def done(self):
        return isinstance(self.now, tuple)

    def marker(self):
        return self.now[0] if self.done() else self.now


def shards(
    size, tokens, cotangent, lengths, w_query, w_key, w_value, w_out, attn_gain, w_gate, w_up, w_down,
    mlp_gain,
):
    count, width = tokens.shape
    kv = KVH * HD
    rows = w_query.shape[0]
    quarter = rows // 2
    hidden = w_gate.shape[1]
    part = w_down.shape[0]
    lane = 128
    all_steps = part // lane
    steps = (all_steps * 2 // 3, all_steps - all_steps * 2 // 3)
    chunk = 6 * lane
    rep = lax.axis_index("rep")
    shard = lax.axis_index("shard")
    core = rep % 2
    ids = jnp.stack([shard, core]).astype(jnp.int32)
    bits = size.bit_length() - 1

    def over_x(value):
        return lax.ppermute(value, "shard", [(0, 1), (1, 0)])

    def over_rep(value, bit):
        return lax.ppermute(value, "rep", [(i, i ^ (1 << bit)) for i in range(size)])

    def pick(value, axis, index, total):
        step = value.shape[axis] // total
        return lax.dynamic_slice_in_dim(value, index * step, step, axis)

    tok = tokens.T
    cot = cotangent.T
    down = w_down.T
    params = pltpu.CompilerParams(vmem_limit_bytes=56 * MIB)
    packed = pl.pallas_call(
        pack_first_kernel,
        out_shape=shape((quarter + 16, width + 2 * kv), BF16),
        in_specs=vmem(5),
        out_specs=pl.BlockSpec(memory_space=pltpu.VMEM),
        cost_estimate=cost(2),
        name="pack_first",
    )(w_query, w_key, w_value, attn_gain, mlp_gain)
    second, third = pl.pallas_call(
        pack_rest_kernel,
        out_shape=(
            shape((quarter, (steps[0] + 1) * chunk), BF16),
            shape((quarter, steps[1] * chunk), BF16),
        ),
        in_specs=[SMEM] + vmem(4),
        out_specs=vmem(2),
        compiler_params=params,
        cost_estimate=cost(3),
        name="pack_rest",
    )(after(ids, packed), w_gate, w_up, down, w_out)
    ends = jnp.cumsum(lengths[0], dtype=jnp.int32)
    begins = ends - lengths[0]
    row_ids = jnp.arange(count, dtype=jnp.int32)
    starts = jnp.max(jnp.where(row_ids[None, :] >= begins[:, None], begins[:, None], 0), axis=0)
    offset = (row_ids - starts).astype(F32)
    frequency = THETA ** (-2.0 * jnp.arange(HD // 2, dtype=F32) / HD)
    angles = frequency[:, None] * offset[None, :]
    cos = jnp.cos(angles)
    sin = jnp.sin(angles)
    at = jnp.arange(count // BLOCK, dtype=jnp.int32)
    first = jnp.max(jnp.where(at[:, None] * BLOCK >= begins[None, :], begins[None, :], 0), axis=1)
    need = (at + 1) * (BLOCK // STRIP) - first // STRIP
    starts = starts[None, :]

    first_a = after(over_x(packed), second, cos, sin, starts, need)
    first_b = over_rep(first_a, 0)
    second = after(second, first_a)

    w_full, gains, normed, q, k, v = pl.pallas_call(
        project_kernel,
        out_shape=(
            shape((width, width + 2 * kv), BF16),
            shape((width, 8), F32),
            shape((width, count), BF16),
            shape((width, count), BF16),
            shape((kv, count), BF16),
            shape((kv, count), BF16),
        ),
        in_specs=[SMEM] + vmem(9),
        out_specs=vmem(6),
        compiler_params=params,
        cost_estimate=cost(5),
        name="project",
    )(after(ids, second), tok, w_query, w_key, w_value, packed, first_a, first_b, cos, sin)

    def one(size_of, index):
        return pl.BlockSpec((size_of, count), lambda i: (index, 0))

    atts, lows, lses = [], [], []
    for g in range(KVH):
        att, low, lse = pl.pallas_call(
            attend_kernel,
            grid=(1,),
            out_shape=(shape((GQ, count), F32), shape((GQ, count), BF16), shape((8, count), F32)),
            in_specs=[SMEM, one(1, 0), one(GQ, g), one(HD, g), one(HD, g)],
            out_specs=(one(GQ, 0), one(GQ, 0), one(8, 0)),
            scratch_shapes=[pltpu.VMEM((count, HD), BF16)],
            compiler_params=params,
            cost_estimate=cost(7),
            name="attend",
        )(after(need, *lses[-1:]), starts, q, k, v)
        atts.append(att)
        lows.append(low)
        lses.append(lse)

    second_a = after(over_x(second), lses[-1])
    third = after(third, second_a)
    second_b = over_rep(second_a, 0)

    def whole(dims):
        return pl.BlockSpec(dims, lambda i: (0,) * len(dims))

    def hidden_specs(turn):
        begin = turn * steps[0]
        low = pl.BlockSpec((rows, lane), lambda i: (0, begin + i))
        high = pl.BlockSpec((rows, lane), lambda i: (0, all_steps + begin + i))
        return [
            low, high, low, high,
            pl.BlockSpec((width, lane), lambda i: (0, begin + i)),
            pl.BlockSpec((quarter, chunk), lambda i: (0, i)),
            pl.BlockSpec((quarter, chunk), lambda i: (0, i)),
        ]

    wide = whole((width, count))
    anywhere = pl.BlockSpec(memory_space=pl.ANY)
    att_specs = [whole((GQ, count))] * KVH
    grad_shapes = [
        shape((quarter, chunk * steps[0]), BF16),
        shape((quarter, chunk * (steps[1] + 1)), BF16),
    ]
    weight_scratch = [pltpu.VMEM((width, 2 * lane), BF16)] * 3 + [pltpu.VMEM((count, width), BF16)] * 2
    wo_spec = pl.BlockSpec((quarter, chunk), lambda i: (0, steps[0]))
    mid, nm, acc_out, acc_e, wo, *grads_1 = pl.pallas_call(
        middle_first_kernel,
        grid=(steps[0],),
        out_shape=(
            shape((width, count), F32),
            shape((width, count), BF16),
            shape((width, count), F32),
            shape((width, count), F32),
            shape((width, width), BF16),
            *[grad_shapes[0]] * 4,
        ),
        in_specs=[SMEM, wide, wide] + att_specs
        + [whole((width, 8)), whole((rows, width)), wo_spec, wo_spec] + hidden_specs(0),
        out_specs=(anywhere, anywhere, wide, wide, anywhere) + (anywhere,) * 4,
        scratch_shapes=weight_scratch
        + [
            pltpu.VMEM((width, count), F32),
            pltpu.VMEM((width, count), BF16),
            pltpu.VMEM((width, width), BF16),
            pltpu.VMEM((4, *grad_shapes[0].shape), BF16),
            pltpu.SemaphoreType.DMA((3,)),
            pltpu.SemaphoreType.DMA((4,)),
        ],
        compiler_params=params,
        cost_estimate=cost(18),
        name="middle_first",
    )(
        after(ids, third), tok, cot, *lows, gains, w_out, second_a, second_b,
        w_gate, w_gate, w_up, w_up, down, second_a, second_b,
    )

    def half_of(total, bit, axis):
        side = (rep >> bit) % 2
        return pick(total, axis, side, 2), pick(total, axis, 1 - side, 2)

    def join(total, got, bit, axis):
        side = (rep >> bit) % 2
        return jnp.where(
            side == 0,
            jnp.concatenate([total, got], axis=axis),
            jnp.concatenate([got, total], axis=axis),
        )

    def reduce_steps(stay, leave, send_stay, send_leave, cuts):
        def end(value, marker):
            return value if marker is None else after(value, marker)

        marker = yield send_leave
        sent = leave + end(over_rep(send_leave, 0), marker)
        stay = stay + over_rep(after(send_stay, sent), 0)
        marker = yield sent
        total = stay + end(over_x(sent), marker)
        done = []
        for bit in range(1, bits):
            if bit in cuts:
                stay, sent = half_of(total, bit, cuts[bit])
                done.append(bit)
            else:
                stay = sent = total
            marker = yield sent
            total = stay + end(over_rep(sent, bit), marker)
        for bit in reversed(done):
            marker = yield total
            total = join(total, end(over_rep(total, bit), marker), bit, cuts[bit])
        marker = yield total
        yield total, end(over_rep(total, 0), marker)

    third_a = after(over_x(third), mid)
    third_b = over_rep(third_a, 0)
    run_1 = Stages(reduce_steps(*grads_1[:3], after(grads_1[3], third_a), {1: 0, 2: 1}))
    out, d_mid, d_att, *grads_2 = pl.pallas_call(
        middle_second_kernel,
        grid=(steps[1],),
        out_shape=(
            shape((width, count), BF16),
            shape((width, count), F32),
            shape((width, count), BF16),
            *[grad_shapes[1]] * 4,
        ),
        in_specs=[SMEM, wide, wide, whole((width, 8))] + [anywhere] * (KVH + 4) + hidden_specs(1),
        out_specs=(
            *[anywhere] * 7,
        ),
        scratch_shapes=weight_scratch
        + [pltpu.VMEM((width, count), F32)] * 2
        + [pltpu.VMEM((width, count), BF16), pltpu.VMEM((width, width), BF16)]
        + [pltpu.VMEM((width, count), F32)] * 3
        + [pltpu.VMEM((width, count), BF16)] * 2
        + [pltpu.VMEM((4, *grad_shapes[1].shape), BF16)]
        + [pltpu.SemaphoreType.DMA((10,)), pltpu.SemaphoreType.DMA((4,))],
        compiler_params=params,
        cost_estimate=cost(18),
        name="middle_second",
    )(
        after(ids, run_1.step()), cot, nm, gains, *lows, wo, mid, acc_out, acc_e,
        w_gate, w_gate, w_up, w_up, down, third_a, third_b,
    )
    run_2 = Stages(reduce_steps(*grads_2, {1: 0, 2: 1}))
    sent = [run_1.step(d_mid), run_2.step()]

    d_parts, earlier = [], []
    for g in range(KVH):
        joined = earlier if g == KVH - 1 else []
        grads_to = [(quarter, GD * KVH)] * 4 if joined else [(4, quarter, GD)]
        d_part, *pair = pl.pallas_call(
            attend_back_kernel,
            grid=(1,),
            out_shape=(
                shape((GD, count), BF16),
                *[shape(dims, BF16) for dims in grads_to],
            ),
            in_specs=[
                SMEM, SMEM, one(1, 0), one(GQ, g), one(HD, g), one(HD, g), one(GQ, g), one(GQ, 0),
                one(8, 0), one(HD // 2, 0), one(HD // 2, 0), one(width, 0),
            ] + [whole(x.shape) for x in joined],
            out_specs=(one(GD, 0), *[whole(dims) for dims in grads_to]),
            scratch_shapes=[pltpu.VMEM((HD, count), F32)] * 2 + [pltpu.VMEM((count, HD), BF16)] * 2,
            compiler_params=params,
            cost_estimate=cost(10),
            name="attend_back",
        )(
            after(ids, *sent), need, starts, q, k, v, d_att, atts[g], lses[g],
            cos, sin, normed, *joined,
        )
        d_parts.append(d_part)
        earlier += pair
        sent = [run_1.step(d_part), run_2.step(d_part)]
    run_3 = Stages(reduce_steps(*pair[:3], after(pair[3], *sent), {1: 0}))
    sent.append(run_3.step())

    d_tok = pl.pallas_call(
        input_kernel,
        out_shape=shape((width, count), F32),
        in_specs=vmem(7),
        out_specs=pl.BlockSpec(memory_space=pltpu.VMEM),
        scratch_shapes=[pltpu.VMEM((width + 2 * kv, count), BF16)],
        compiler_params=params,
        cost_estimate=cost(7),
        name="input_grad",
    )(after(tok, *sent), d_mid, w_full, gains, *d_parts)

    sent = run_3.step(d_tok)
    run_1.step(after(d_tok, sent))
    run_2.step(after(d_tok, sent))
    sent = run_3.step()
    run_1.step(sent)
    run_2.step(sent)
    sent = run_3.step()
    run_1.step(sent)
    run_3.step()
    sent = run_3.step()
    while not (run_1.done() and run_2.done()):
        run_1.step(sent)
        run_2.step(sent)
    gain_shape = shape((rows,), F32)
    grad_gate, grad_up, grad_down, grad_out, grad_mlp_gain = pl.pallas_call(
        finish_hidden_kernel,
        out_shape=(
            shape((rows, hidden), F32), shape((rows, hidden), F32), shape((width, part), F32),
            shape((rows, width), F32), gain_shape,
        ),
        in_specs=[SMEM] + vmem(7),
        out_specs=vmem(5),
        compiler_params=params,
        cost_estimate=cost(5),
        name="finish_hidden",
    )(after(ids, sent), *run_1.now, *run_2.now, w_gate, w_up, gains)
    run_3.step(grad_mlp_gain)
    while not run_3.done():
        run_3.step()
    grad_query, grad_key, grad_value, grad_attn_gain = pl.pallas_call(
        finish_last_kernel,
        out_shape=(
            shape((rows, width), F32), shape((rows, kv), F32), shape((rows, kv), F32), gain_shape
        ),
        in_specs=[SMEM] + vmem(6),
        out_specs=vmem(4),
        compiler_params=params,
        cost_estimate=cost(3),
        name="finish_last",
    )(ids, *run_3.now, w_query, w_key, w_value, gains)
    grad_down = grad_down.T
    return (
        out.T, d_tok.T, grad_query, grad_key, grad_value, grad_out, grad_attn_gain,
        grad_gate, grad_up, grad_down, grad_mlp_gain,
    )


def solution(mesh):
    everywhere = P(("rep", "shard"), None)
    weight = P("shard", None)
    gain = P("shard")
    return jax.shard_map(
        functools.partial(shards, mesh.shape["rep"]),
        mesh=mesh,
        in_specs=(
            everywhere, everywhere, everywhere, weight, weight, weight, weight, gain, weight, weight,
            weight, gain,
        ),
        out_specs=(
            everywhere, everywhere, weight, weight, weight, weight, gain, weight, weight, weight, gain,
        ),
        check_vma=False,
    )
```

```python
import functools

import jax
import jax.numpy as jnp
from jax import lax
from jax.experimental import pallas as pl
from jax.experimental.pallas import tpu as pltpu
from jax.sharding import PartitionSpec as P

H = 9
KVH = 3
HD = 64
MAXLEN = 512
EPS = 1e-05
THETA = 100000.0
BLOCK = 256
STRIP = 128
GROUPS = H // KVH
GQ = GROUPS * HD
GD = GQ + 2 * HD
SCALE = HD ** (-0.5)
F32 = jnp.float32
BF16 = jnp.bfloat16
MIB = 1024 * 1024


def dot_nn(left, right):
    return lax.dot_general(left, right, (((1,), (0,)), ((), ())), preferred_element_type=F32)


def dot_nt(left, right):
    return lax.dot_general(left, right, (((1,), (1,)), ((), ())), preferred_element_type=F32)


def dot_tn(left, right):
    return lax.dot_general(left, right, (((0,), (0,)), ((), ())), preferred_element_type=F32)


def put_rows(full, own, got_a, got_b, shard, core):
    rows = own.shape[0]
    half = rows // 2
    full[pl.ds(pl.multiple_of(shard * rows, 16), rows), :] = own[...]
    other = (1 - shard) * rows
    full[pl.ds(pl.multiple_of(other + core * half, 16), half), :] = got_a[...]
    full[pl.ds(pl.multiple_of(other + (1 - core) * half, 16), half), :] = got_b[...]


def pack_first_kernel(wq, wk, wv, attn_gain, mlp_gain, packed):
    core = lax.axis_index("rep") % 2
    rows, width = wq.shape
    part = rows // 2
    half = pl.ds(pl.multiple_of(core * part, 16), part)
    packed[:part, :width] = wq[half, :]
    packed[:part, width : width + KVH * HD] = wk[half, :]
    packed[:part, width + KVH * HD :] = wv[half, :]
    row = lax.broadcasted_iota(jnp.int32, (packed.shape[0] - part, rows), 0)
    first = attn_gain[...].astype(F32).reshape(1, rows)
    second = mlp_gain[...].astype(F32).reshape(1, rows)
    packed[part:, :rows] = jnp.where(row == 0, first, jnp.where(row == 1, second, 0.0)).astype(BF16)


def pack_rest_kernel(ids, wg, wu, wd, wo, packed_0, packed_1):
    core = ids[1]
    rows = wg.shape[0]
    part = rows // 2
    lane = 128
    shift = wg.shape[1] // 2
    steps = packed_1.shape[1] // (6 * lane)
    first = shift // lane - steps
    half = pl.ds(pl.multiple_of(core * part, 16), part)
    for packed, begin, end in ((packed_0, 0, first), (packed_1, first, first + steps)):
        for step in range(begin, end):
            low = slice(step * lane, (step + 1) * lane)
            high = slice(shift + low.start, shift + low.stop)
            to = (step - begin) * 6 * lane
            for at, (source, columns) in enumerate(((wg, low), (wg, high), (wu, low), (wu, high))):
                packed[:, to + at * lane : to + (at + 1) * lane] = source[half, columns]
            for side in range(2):
                down = pl.ds(pl.multiple_of(core * rows + side * part, 16), part)
                packed[:, to + (4 + side) * lane : to + (5 + side) * lane] = wd[down, low]
    to = first * 6 * lane
    packed_0[:, to : to + wo.shape[1]] = wo[half, :]


def project_kernel(
    ids, tok, wq, wk, wv, packed, got_a, got_b, cos, sin,
    w_full, gains, normed, q_out, k_out, v_out,
):
    shard, core = ids[0], ids[1]
    rows = wq.shape[0]
    own = pl.ds(pl.multiple_of(shard * rows, 16), rows)
    part = rows // 2
    other = (1 - shard) * rows
    w_full[own, : wq.shape[1]] = wq[...]
    w_full[own, wq.shape[1] : wq.shape[1] + KVH * HD] = wk[...]
    w_full[own, wq.shape[1] + KVH * HD :] = wv[...]
    w_full[pl.ds(pl.multiple_of(other + core * part, 16), part), :] = got_a[:part, :]
    w_full[pl.ds(pl.multiple_of(other + (1 - core) * part, 16), part), :] = got_b[:part, :]
    lanes = (rows + 127) // 128 * 128
    gains[own, :] = packed[part:, :lanes].astype(F32).T[:rows, :8]
    gains[pl.ds(pl.multiple_of(other, 16), rows), :] = got_a[part:, :lanes].astype(F32).T[:rows, :8]
    width, count = tok.shape
    kv = KVH * HD
    half = HD // 2
    gain = gains[:, 0:1]
    for at in range(0, count, BLOCK):
        lanes = slice(at, at + BLOCK)
        x = tok[:, lanes].astype(F32)
        r = lax.rsqrt(jnp.mean(x * x, axis=0, keepdims=True) + EPS)
        normed[:, lanes] = (x * r * gain).astype(BF16)
    for at in range(0, count, BLOCK):
        lanes = slice(at, at + BLOCK)
        pre = dot_tn(w_full[...], normed[:, lanes])
        c = cos[:, lanes]
        s = sin[:, lanes]
        for head in range(H + KVH):
            row = head * HD
            a = pre[row : row + half]
            b = pre[row + half : row + HD]
            front = a * c - b * s
            back = b * c + a * s
            if head < H:
                q_out[row : row + half, lanes] = (front * SCALE).astype(BF16)
                q_out[row + half : row + HD, lanes] = (back * SCALE).astype(BF16)
            else:
                row -= width
                k_out[row : row + half, lanes] = front.astype(BF16)
                k_out[row + half : row + HD, lanes] = back.astype(BF16)
        v_out[:, lanes] = pre[width + kv :].astype(BF16)


def side_by_side(ref, lanes, rows=HD):
    return jnp.concatenate([ref[j * rows : (j + 1) * rows, lanes] for j in range(GROUPS)], axis=1)


def span_of(at, strips):
    return pl.ds(pl.multiple_of((at + 1) * BLOCK - strips * STRIP, STRIP), strips * STRIP)


def window(at, strips, starts):
    rows = lax.broadcasted_iota(jnp.int32, (strips * STRIP, GROUPS * BLOCK), 0)
    rows += span_of(at, strips).start
    columns = at * BLOCK + lax.broadcasted_iota(jnp.int32, (1, BLOCK), 1)
    starts = jnp.concatenate([starts] * GROUPS, axis=1)
    columns = jnp.concatenate([columns] * GROUPS, axis=1)
    return (rows >= starts) & (rows <= columns)


def reaches(count):
    own = BLOCK // STRIP
    return range(own, min(count // STRIP, own + (MAXLEN + STRIP - 2) // STRIP) + 1)


def attend_kernel(need, starts, q, k, v, att, att_low, lse, k_rows):
    count = q.shape[1]
    k_rows[...] = k[...].T

    @pl.loop(0, count // BLOCK)
    def _(at):
        lanes = pl.ds(pl.multiple_of(at * BLOCK, BLOCK), BLOCK)
        for strips in reaches(count):

            @pl.when(need[at] == strips)
            def _(strips=strips):
                ok = window(at, strips, starts[:, lanes])
                span = span_of(at, strips)
                scores = jnp.where(ok, dot_nn(k_rows[span, :], side_by_side(q, lanes)), -1e30)
                top = jnp.max(scores, axis=0, keepdims=True)
                e = jnp.exp(scores - top)
                total = jnp.sum(e, axis=0, keepdims=True)
                o = dot_nn(v[:, span], e.astype(BF16)) / total
                logs = top + jnp.log(total)
                for j in range(GROUPS):
                    rows = slice(j * HD, (j + 1) * HD)
                    one = slice(j * BLOCK, (j + 1) * BLOCK)
                    att[rows, lanes] = o[:, one]
                    att_low[rows, lanes] = o[:, one].astype(BF16)
                    lse[j : j + 1, lanes] = logs[:, one]


def place(target, shard, core, x, c, columns, value):
    away = jnp.where(core == c, 0, 2) + jnp.where(shard == x, 0, 1)
    target[away, :, columns] = value


def hidden_step(
    ids, cot, cot_rows, nm, nm_rows, acc_out, acc_e,
    wg_lo, wg_hi, wu_lo, wu_hi, wd_own, got_a, got_b, grads, wg, wu, wd, base,
):
    shard, core = ids[0], ids[1]
    width = cot.shape[0]
    rows, lane = wg_lo.shape
    half = rows // 2
    own = pl.ds(pl.multiple_of(shard * rows, 16), rows)
    other = (1 - shard) * rows
    at_a = pl.ds(pl.multiple_of(other + core * half, 16), half)
    at_b = pl.ds(pl.multiple_of(other + (1 - core) * half, 16), half)
    wg[own, :lane] = wg_lo[...]
    wg[own, lane:] = wg_hi[...]
    wu[own, :lane] = wu_lo[...]
    wu[own, lane:] = wu_hi[...]
    for at, got in ((at_a, got_a), (at_b, got_b)):
        wg[at, :] = got[:, : 2 * lane]
        wu[at, :] = got[:, 2 * lane : 4 * lane]
    for turn in range(2):

        @pl.when(shard == turn)
        def _(turn=turn):
            wd[:, turn * lane : (turn + 1) * lane] = wd_own[...]
            columns = slice((1 - turn) * lane, (2 - turn) * lane)
            for side in range(2):
                from_a = pl.ds(pl.multiple_of(core * rows + side * half, 16), half)
                from_b = pl.ds(pl.multiple_of((1 - core) * rows + side * half, 16), half)
                source = slice((4 + side) * lane, (5 + side) * lane)
                wd[from_a, columns] = got_a[:, source]
                wd[from_b, columns] = got_b[:, source]

    gate = dot_nn(nm_rows[...], wg[...])
    up = dot_nn(nm_rows[...], wu[...])
    dh = dot_nn(cot_rows[...], wd[...])
    sg = jax.nn.sigmoid(gate)
    sw = gate * sg
    hid = (sw * up).astype(BF16)
    dg = (dh * up * sg * (1.0 + gate * (1.0 - sg))).astype(BF16)
    du = (dh * sw).astype(BF16)
    acc_out[...] += dot_nt(wd[...], hid)
    acc_e[...] += dot_nt(wg[...], dg) + dot_nt(wu[...], du)
    g_gate = dot_nn(nm[...], dg).astype(BF16)
    g_up = dot_nn(nm[...], du).astype(BF16)
    g_down = dot_nn(cot[...], hid).astype(BF16)
    for x in range(2):
        for c in range(2):
            first = (2 * x + c) * half
            at_gate = pl.ds(pl.multiple_of(base, lane), 2 * lane)
            at_up = pl.ds(pl.multiple_of(base + 2 * lane, lane), 2 * lane)
            place(grads, shard, core, x, c, at_gate, g_gate[first : first + half])
            place(grads, shard, core, x, c, at_up, g_up[first : first + half])
            for side in range(2):
                first = c * rows + side * half
                value = g_down[first : first + half, x * lane : (x + 1) * lane]
                columns = pl.ds(pl.multiple_of(base + (4 + side) * lane, lane), lane)
                place(grads, shard, core, x, c, columns, value)


def middle_first_kernel(
    ids, tok, cot, att, gains, wo_own, wo_a, wo_b,
    wg_lo, wg_hi, wu_lo, wu_hi, wd_own, got_a, got_b,
    mid_out, nm_out, acc_out, acc_e, wo_out, grads_0, grads_1, grads_2, grads_3,
    wg, wu, wd, nm_rows, cot_rows, mid, nm, wo, grads, sems, grad_sems,
):
    step = pl.program_id(0)
    block = 6 * wg_lo.shape[1]
    columns = pl.ds(pl.multiple_of(step * block, 128), block)
    outs = (grads_0, grads_1, grads_2, grads_3)
    leave = [
        pltpu.make_async_copy(grads.at[at, :, columns], out.at[:, columns], grad_sems.at[at])
        for at, out in enumerate(outs)
    ]
    copies = [
        pltpu.make_async_copy(source, target, sems.at[at])
        for at, (source, target) in enumerate(((mid, mid_out), (nm, nm_out), (wo, wo_out)))
    ]

    @pl.when(step == 0)
    def _():
        width = wo.shape[0]
        put_rows(wo, wo_own, wo_a.at[:, :width], wo_b.at[:, :width], ids[0], ids[1])
        copies[2].start()
        gain = gains[:, 1:2]
        mid[...] = tok[...].astype(F32) + dot_tn(wo[...], att[...])
        copies[0].start()
        for at in range(0, tok.shape[1], BLOCK):
            lanes = slice(at, at + BLOCK)
            m = mid[:, lanes]
            r = lax.rsqrt(jnp.mean(m * m, axis=0, keepdims=True) + EPS)
            part = (m * r * gain).astype(BF16)
            nm[:, lanes] = part
            nm_rows[lanes, :] = part.T
            cot_rows[lanes, :] = cot[:, lanes].T
        copies[1].start()
        acc_out[...] = jnp.zeros_like(acc_out)
        acc_e[...] = jnp.zeros_like(acc_e)

    hidden_step(
        ids, cot, cot_rows, nm, nm_rows, acc_out, acc_e,
        wg_lo, wg_hi, wu_lo, wu_hi, wd_own, got_a, got_b, grads, wg, wu, wd, step * block,
    )

    for copy in leave:
        copy.start()

    @pl.when(step == pl.num_programs(0) - 1)
    def _():
        for copy in copies:
            copy.wait()
        for at, out in enumerate(outs):
            pltpu.make_async_copy(grads.at[at], out, grad_sems.at[at]).wait()


def middle_second_kernel(
    ids, cot, nm, gains, att_in, wo_in, mid_in, out_in, e_in,
    wg_lo, wg_hi, wu_lo, wu_hi, wd_own, got_a, got_b,
    out_out, d_mid_out, d_att_out, grads_0, grads_1, grads_2, grads_3,
    wg, wu, wd, nm_rows, cot_rows, acc_out, acc_e, att, wo, mid, out_first, e_first, out, d_att, grads,
    sems, grad_sems,
):
    step = pl.program_id(0)
    arrive = [
        (att_in, att), (wo_in, wo), (mid_in, mid), (out_in, out_first), (e_in, e_first),
    ]
    arrive = [pltpu.make_async_copy(*pair, sems.at[at]) for at, pair in enumerate(arrive)]
    leave = [(out, out_out), (mid, d_mid_out), (d_att, d_att_out)]
    leave = [pltpu.make_async_copy(*pair, sems.at[len(arrive) + at]) for at, pair in enumerate(leave)]
    grads_leave = [
        pltpu.make_async_copy(grads.at[at], out_at, grad_sems.at[at])
        for at, out_at in enumerate((grads_0, grads_1, grads_2, grads_3))
    ]

    @pl.when(step == 0)
    def _():
        for copy in arrive:
            copy.start()
        for at in range(0, cot.shape[1], BLOCK):
            lanes = slice(at, at + BLOCK)
            nm_rows[lanes, :] = nm[:, lanes].T
            cot_rows[lanes, :] = cot[:, lanes].T
        acc_out[...] = jnp.zeros_like(acc_out)
        acc_e[...] = jnp.zeros_like(acc_e)

    hidden_step(
        ids, cot, cot_rows, nm, nm_rows, acc_out, acc_e,
        wg_lo, wg_hi, wu_lo, wu_hi, wd_own, got_a, got_b, grads, wg, wu, wd,
        step * (6 * wg_lo.shape[1]),
    )

    @pl.when(step == pl.num_programs(0) - 1)
    def _():
        for copy in arrive:
            copy.wait()
        out[...] = (mid[...] + out_first[...] + acc_out[...]).astype(BF16)
        leave[0].start()
        gain = gains[:, 1:2]
        for at in range(0, cot.shape[1], BLOCK):
            lanes = slice(at, at + BLOCK)
            m = mid[:, lanes]
            r = lax.rsqrt(jnp.mean(m * m, axis=0, keepdims=True) + EPS)
            z = m * r
            e = (e_first[:, lanes] + acc_e[:, lanes]) * gain
            d_part = cot[:, lanes].astype(F32) + r * (e - z * jnp.mean(e * z, axis=0, keepdims=True))
            mid[:, lanes] = d_part
            nm_rows[lanes, :] = d_part.astype(BF16).T
        leave[1].start()
        low = nm_rows[...]
        d_att[...] = dot_nt(wo[...], low).astype(BF16)
        leave[2].start()
        value = dot_nn(att[...], low).astype(BF16)
        half = value.shape[0] // 4
        done = pl.num_programs(0) * 6 * wg_lo.shape[1]
        for x in range(2):
            for c in range(2):
                first = (2 * x + c) * half
                columns = slice(done, done + value.shape[1])
                place(grads, ids[0], ids[1], x, c, columns, value[first : first + half])
        for copy in grads_leave:
            copy.start()
        for copy in leave + grads_leave:
            copy.wait()


def attend_back_kernel(ids, need, starts, q, k, v, d_att, att, lse, cos, sin, normed, *refs):
    *refs, dk_acc, dv_acc, k_rows, v_rows = refs
    *earlier, d_out = refs[: len(refs) - (4 if len(refs) > 2 else 1)]
    targets = refs[len(earlier) + 1 :]
    count = q.shape[1]
    half = HD // 2
    k_rows[...] = k[...].T
    v_rows[...] = v[...].T
    dk_acc[...] = jnp.zeros_like(dk_acc)
    dv_acc[...] = jnp.zeros_like(dv_acc)

    @pl.loop(0, count // BLOCK)
    def _(at):
        lanes = pl.ds(pl.multiple_of(at * BLOCK, BLOCK), BLOCK)
        for strips in reaches(count):

            @pl.when(need[at] == strips)
            def _(strips=strips):
                ok = window(at, strips, starts[:, lanes])
                span = span_of(at, strips)
                c = cos[:, lanes]
                s = sin[:, lanes]
                q_part = side_by_side(q, lanes)
                d_part = side_by_side(d_att, lanes)
                scores = jnp.where(ok, dot_nn(k_rows[span, :], q_part), -1e30)
                probs = jnp.exp(scores - side_by_side(lse, lanes, 1))
                d_probs = dot_nn(v_rows[span, :], d_part)
                centre = jnp.sum(
                    d_part.astype(F32) * side_by_side(att, lanes), axis=0, keepdims=True
                )
                d_scores = (probs * (d_probs - centre)).astype(BF16)
                dq = dot_nn(k[:, span], d_scores) * SCALE
                for j in range(GROUPS):
                    one = slice(j * BLOCK, (j + 1) * BLOCK)
                    a = dq[:half, one]
                    b = dq[half:, one]
                    d_out[j * HD : j * HD + half, lanes] = (a * c + b * s).astype(BF16)
                    d_out[j * HD + half : (j + 1) * HD, lanes] = (b * c - a * s).astype(BF16)
                dk_acc[:, span] += dot_nt(q_part, d_scores)
                dv_acc[:, span] += dot_nt(d_part, probs.astype(BF16))
    a = dk_acc[:half, :]
    b = dk_acc[half:, :]
    d_out[GQ : GQ + half, :] = (a * cos[...] + b * sin[...]).astype(BF16)
    d_out[GQ + half : GQ + HD, :] = (b * cos[...] - a * sin[...]).astype(BF16)
    d_out[GQ + HD :, :] = dv_acc[...].astype(BF16)
    value = dot_nt(normed[...], d_out[...]).astype(BF16)
    quarter = value.shape[0] // 4
    for x in range(2):
        for c in range(2):
            first = (2 * x + c) * quarter
            part = value[first : first + quarter]
            if not earlier:
                place(targets[0], ids[0], ids[1], x, c, slice(None), part)
            for away, target in enumerate(targets if earlier else []):

                @pl.when((away // 2 == (ids[1] ^ c)) & (away % 2 == (ids[0] ^ x)))
                def _(target=target, part=part):
                    target[:, len(earlier) * GD :] = part

    for at, group in enumerate(earlier):
        for away, target in enumerate(targets):
            target[:, at * GD : (at + 1) * GD] = group[away]


def input_kernel(tok, d_mid, w_full, gains, d_0, d_1, d_2, d_tok, d_all):
    width, count = tok.shape
    kv = KVH * HD
    for g, part in enumerate((d_0, d_1, d_2)):
        d_all[g * GQ : (g + 1) * GQ, :] = part[:GQ, :]
        d_all[width + g * HD : width + (g + 1) * HD, :] = part[GQ : GQ + HD, :]
        d_all[width + kv + g * HD : width + kv + (g + 1) * HD, :] = part[GQ + HD :, :]
    gain = gains[:, 0:1]
    for at in range(0, count, BLOCK):
        lanes = slice(at, at + BLOCK)
        x = tok[:, lanes].astype(F32)
        r = lax.rsqrt(jnp.mean(x * x, axis=0, keepdims=True) + EPS)
        z = x * r
        e = dot_nn(w_full[...], d_all[:, lanes]) * gain
        d_tok[:, lanes] = d_mid[:, lanes] + r * (e - z * jnp.mean(e * z, axis=0, keepdims=True))


def row_of(column):
    rows = column.shape[0]
    lanes = (rows + 127) // 128 * 128
    wide = jnp.broadcast_to(column, (rows, 128))
    return jnp.concatenate([wide, jnp.zeros((lanes - rows, 128), F32)], axis=0).T[0, :rows]


def finish_hidden_kernel(
    ids, mine_1, got_1, mine_2, got_2, wg, wu, gains, gate, up, down, g_out, gain_out
):
    shard, core = ids[0], ids[1]
    rows, hidden = wg.shape
    half = rows // 2
    lane = 128
    steps = mine_1.shape[1] // (6 * lane)
    total_steps = hidden // 2 // lane
    sums = []
    for parts, side_of in (((mine_1, mine_2), core), ((got_1, got_2), 1 - core)):
        at = pl.ds(pl.multiple_of(side_of * half, 16), half)
        total = jnp.zeros((half, lane), F32)
        done = (total_steps - steps) * 6 * lane
        g_out[at, :] = parts[1][:, done : done + g_out.shape[1]].astype(F32)
        for turn, turn_steps in enumerate((steps, total_steps - steps)):
            for step in range(turn_steps):
                low = (turn * steps + step) * lane
                begin = step * 6 * lane
                for high in range(2):
                    columns = slice(high * hidden // 2 + low, high * hidden // 2 + low + lane)
                    g = parts[turn][:, begin + high * lane : begin + (high + 1) * lane].astype(F32)
                    u = parts[turn][:, begin + (2 + high) * lane : begin + (3 + high) * lane].astype(F32)
                    gate[at, columns] = g
                    up[at, columns] = u
                    total += wg[at, columns].astype(F32) * g + wu[at, columns].astype(F32) * u
                for side in range(2):
                    d = parts[turn][:, begin + (4 + side) * lane : begin + (5 + side) * lane]
                    to = pl.ds(pl.multiple_of(side_of * rows + side * half, 16), half)
                    down[to, low : low + lane] = d.astype(F32)
        sums.append((at, jnp.sum(total, axis=1, keepdims=True)))
    own = pl.ds(pl.multiple_of(shard * rows, 16), rows)
    gain = gains[own, 1:2]
    first = jnp.where(core == 0, sums[0][1], sums[1][1])
    second = jnp.where(core == 0, sums[1][1], sums[0][1])
    gain_out[...] = row_of(jnp.concatenate([first, second], axis=0) / gain)


def finish_last_kernel(ids, mine, got, wq, wk, wv, gains, g_query, g_key, g_value, gain_out):
    shard, core = ids[0], ids[1]
    rows = wq.shape[0]
    half = rows // 2
    sums = []
    for part, side_of in ((mine, core), (got, 1 - core)):
        at = pl.ds(pl.multiple_of(side_of * half, 16), half)
        total = jnp.zeros((half, 1), F32)
        for weight, grad, begin, length in (
            (wq, g_query, 0, GQ), (wk, g_key, GQ, HD), (wv, g_value, GQ + HD, HD)
        ):
            pieces = [
                part[:, g * GD + begin : g * GD + begin + length] for g in range(KVH)
            ]
            value = jnp.concatenate(pieces, axis=1).astype(F32)
            grad[at, :] = value
            total += jnp.sum(weight[at, :].astype(F32) * value, axis=1, keepdims=True)
        sums.append(total)
    own = pl.ds(pl.multiple_of(shard * rows, 16), rows)
    gain = gains[own, 0:1]
    first = jnp.where(core == 0, sums[0], sums[1])
    second = jnp.where(core == 0, sums[1], sums[0])
    gain_out[...] = row_of(jnp.concatenate([first, second], axis=0) / gain)


SMEM = pl.BlockSpec(memory_space=pltpu.SMEM)


def cost(microseconds):
    return pl.CostEstimate(flops=microseconds * 10**9, bytes_accessed=MIB, transcendentals=0)


def vmem(count):
    return [pl.BlockSpec(memory_space=pltpu.VMEM)] * count


def shape(dims, dtype):
    return jax.ShapeDtypeStruct(dims, dtype)


def after(value, *others):
    return lax.optimization_barrier((value, *others))[0]


class Stages:
    def __init__(self, stages):
        self.stages = stages
        self.now = next(stages)

    def step(self, marker=None):
        if not self.done():
            self.now = self.stages.send(marker)
        return self.marker()

    def done(self):
        return isinstance(self.now, tuple)

    def marker(self):
        return self.now[0] if self.done() else self.now


def shards(
    size, tokens, cotangent, lengths, w_query, w_key, w_value, w_out, attn_gain, w_gate, w_up, w_down,
    mlp_gain,
):
    count, width = tokens.shape
    kv = KVH * HD
    rows = w_query.shape[0]
    quarter = rows // 2
    hidden = w_gate.shape[1]
    part = w_down.shape[0]
    lane = 128
    all_steps = part // lane
    steps = (all_steps * 2 // 3, all_steps - all_steps * 2 // 3)
    chunk = 6 * lane
    rep = lax.axis_index("rep")
    shard = lax.axis_index("shard")
    core = rep % 2
    ids = jnp.stack([shard, core]).astype(jnp.int32)
    bits = size.bit_length() - 1

    def over_x(value):
        return lax.ppermute(value, "shard", [(0, 1), (1, 0)])

    def over_rep(value, bit):
        return lax.ppermute(value, "rep", [(i, i ^ (1 << bit)) for i in range(size)])

    def pick(value, axis, index, total):
        step = value.shape[axis] // total
        return lax.dynamic_slice_in_dim(value, index * step, step, axis)

    tok = tokens.T
    cot = cotangent.T
    down = w_down.T
    params = pltpu.CompilerParams(vmem_limit_bytes=56 * MIB)
    most = pltpu.CompilerParams(vmem_limit_bytes=62 * MIB)
    packed = pl.pallas_call(
        pack_first_kernel,
        out_shape=shape((quarter + 16, width + 2 * kv), BF16),
        in_specs=vmem(5),
        out_specs=pl.BlockSpec(memory_space=pltpu.VMEM),
        cost_estimate=cost(2),
        name="pack_first",
    )(w_query, w_key, w_value, attn_gain, mlp_gain)
    second, third = pl.pallas_call(
        pack_rest_kernel,
        out_shape=(
            shape((quarter, (steps[0] + 1) * chunk), BF16),
            shape((quarter, steps[1] * chunk), BF16),
        ),
        in_specs=[SMEM] + vmem(4),
        out_specs=vmem(2),
        compiler_params=params,
        cost_estimate=cost(3),
        name="pack_rest",
    )(after(ids, packed), w_gate, w_up, down, w_out)
    ends = jnp.cumsum(lengths[0], dtype=jnp.int32)
    begins = ends - lengths[0]
    row_ids = jnp.arange(count, dtype=jnp.int32)
    starts = jnp.max(jnp.where(row_ids[None, :] >= begins[:, None], begins[:, None], 0), axis=0)
    offset = (row_ids - starts).astype(F32)
    frequency = THETA ** (-2.0 * jnp.arange(HD // 2, dtype=F32) / HD)
    angles = frequency[:, None] * offset[None, :]
    cos = jnp.cos(angles)
    sin = jnp.sin(angles)
    at = jnp.arange(count // BLOCK, dtype=jnp.int32)
    first = jnp.max(jnp.where(at[:, None] * BLOCK >= begins[None, :], begins[None, :], 0), axis=1)
    need = (at + 1) * (BLOCK // STRIP) - first // STRIP
    starts = starts[None, :]

    first_a = after(over_x(packed), second, cos, sin, starts, need)
    first_b = over_rep(first_a, 0)

    w_full, gains, normed, q, k, v = pl.pallas_call(
        project_kernel,
        out_shape=(
            shape((width, width + 2 * kv), BF16),
            shape((width, 8), F32),
            shape((width, count), BF16),
            shape((width, count), BF16),
            shape((kv, count), BF16),
            shape((kv, count), BF16),
        ),
        in_specs=[SMEM] + vmem(9),
        out_specs=vmem(6),
        compiler_params=most,
        cost_estimate=cost(5),
        name="project",
    )(after(ids, second), tok, w_query, w_key, w_value, packed, first_a, first_b, cos, sin)

    def grouped(size_of, first=0):
        return pl.BlockSpec((size_of, count), lambda i: (first + i, 0))

    def shared(size_of):
        return pl.BlockSpec((size_of, count), lambda i: (0, 0))

    att, low, lse = pl.pallas_call(
        attend_kernel,
        grid=(KVH,),
        out_shape=(
            shape((width, count), F32), shape((width, count), BF16), shape((8 * KVH, count), F32)
        ),
        in_specs=[SMEM, shared(1), grouped(GQ), grouped(HD), grouped(HD)],
        out_specs=(grouped(GQ), grouped(GQ), grouped(8)),
        scratch_shapes=[pltpu.VMEM((count, HD), BF16)],
        compiler_params=params,
        cost_estimate=cost(17),
        name="attend",
    )(need, starts, q, k, v)

    second_a = after(over_x(second), lse)
    third = after(third, second_a)
    second_b = over_rep(second_a, 0)

    def whole(dims):
        return pl.BlockSpec(dims, lambda i: (0,) * len(dims))

    def hidden_specs(turn):
        begin = turn * steps[0]
        low = pl.BlockSpec((rows, lane), lambda i: (0, begin + i))
        high = pl.BlockSpec((rows, lane), lambda i: (0, all_steps + begin + i))
        return [
            low, high, low, high,
            pl.BlockSpec((width, lane), lambda i: (0, begin + i)),
            pl.BlockSpec((quarter, chunk), lambda i: (0, i)),
            pl.BlockSpec((quarter, chunk), lambda i: (0, i)),
        ]

    wide = whole((width, count))
    anywhere = pl.BlockSpec(memory_space=pl.ANY)
    grad_shapes = [
        shape((quarter, chunk * steps[0]), BF16),
        shape((quarter, chunk * steps[1] + width), BF16),
    ]
    weight_scratch = [pltpu.VMEM((width, 2 * lane), BF16)] * 3 + [pltpu.VMEM((count, width), BF16)] * 2
    wo_spec = pl.BlockSpec((quarter, chunk), lambda i: (0, steps[0]))
    mid, nm, acc_out, acc_e, wo, *grads_1 = pl.pallas_call(
        middle_first_kernel,
        grid=(steps[0],),
        out_shape=(
            shape((width, count), F32),
            shape((width, count), BF16),
            shape((width, count), F32),
            shape((width, count), F32),
            shape((width, width), BF16),
            *[grad_shapes[0]] * 4,
        ),
        in_specs=[SMEM, wide, wide, wide]
        + [whole((width, 8)), whole((rows, width)), wo_spec, wo_spec] + hidden_specs(0),
        out_specs=(anywhere, anywhere, wide, wide, anywhere) + (anywhere,) * 4,
        scratch_shapes=weight_scratch
        + [
            pltpu.VMEM((width, count), F32),
            pltpu.VMEM((width, count), BF16),
            pltpu.VMEM((width, width), BF16),
            pltpu.VMEM((4, *grad_shapes[0].shape), BF16),
            pltpu.SemaphoreType.DMA((3,)),
            pltpu.SemaphoreType.DMA((4,)),
        ],
        compiler_params=most,
        cost_estimate=cost(18),
        name="middle_first",
    )(
        after(ids, third), tok, cot, low, gains, w_out, second_a, second_b,
        w_gate, w_gate, w_up, w_up, down, second_a, second_b,
    )

    def half_of(total, bit, axis):
        side = (rep >> bit) % 2
        return pick(total, axis, side, 2), pick(total, axis, 1 - side, 2)

    def join(total, got, bit, axis):
        side = (rep >> bit) % 2
        return jnp.where(
            side == 0,
            jnp.concatenate([total, got], axis=axis),
            jnp.concatenate([got, total], axis=axis),
        )

    def reduce_steps(stay, leave, send_stay, send_leave, cuts):
        def end(value, marker):
            return value if marker is None else after(value, marker)

        marker = yield send_leave
        sent = leave + end(over_rep(send_leave, 0), marker)
        stay = stay + over_rep(after(send_stay, sent), 0)
        marker = yield sent
        total = stay + end(over_x(sent), marker)
        done = []
        for bit in range(1, bits):
            if bit in cuts:
                stay, sent = half_of(total, bit, cuts[bit])
                done.append(bit)
            else:
                stay = sent = total
            marker = yield sent
            total = stay + end(over_rep(sent, bit), marker)
        for bit in reversed(done):
            marker = yield total
            total = join(total, end(over_rep(total, bit), marker), bit, cuts[bit])
        marker = yield total
        yield total, end(over_rep(total, 0), marker)

    third_a = after(over_x(third), mid)
    third_b = over_rep(third_a, 0)
    run_1 = Stages(reduce_steps(*grads_1[:3], after(grads_1[3], third_a), {1: 0, 2: 1}))
    out, d_mid, d_att, *grads_2 = pl.pallas_call(
        middle_second_kernel,
        grid=(steps[1],),
        out_shape=(
            shape((width, count), BF16),
            shape((width, count), F32),
            shape((width, count), BF16),
            *[grad_shapes[1]] * 4,
        ),
        in_specs=[SMEM, wide, wide, whole((width, 8))] + [anywhere] * 5 + hidden_specs(1),
        out_specs=(
            *[anywhere] * 7,
        ),
        scratch_shapes=weight_scratch
        + [pltpu.VMEM((width, count), F32)] * 2
        + [pltpu.VMEM((width, count), BF16), pltpu.VMEM((width, width), BF16)]
        + [pltpu.VMEM((width, count), F32)] * 3
        + [pltpu.VMEM((width, count), BF16)] * 2
        + [pltpu.VMEM((4, *grad_shapes[1].shape), BF16)]
        + [pltpu.SemaphoreType.DMA((8,)), pltpu.SemaphoreType.DMA((4,))],
        compiler_params=most,
        cost_estimate=cost(18),
        name="middle_second",
    )(
        after(ids, run_1.step()), cot, nm, gains, low, wo, mid, acc_out, acc_e,
        w_gate, w_gate, w_up, w_up, down, third_a, third_b,
    )
    run_2 = Stages(reduce_steps(*grads_2, {1: 0, 2: 1}))
    sent = [run_1.step(d_mid), run_2.step()]

    def attend_back(group, sent, joined, grad_dims):
        return pl.pallas_call(
            attend_back_kernel,
            grid=(1,),
            out_shape=(shape((GD, count), BF16), *[shape(dims, BF16) for dims in grad_dims]),
            in_specs=[
                SMEM, SMEM, shared(1), grouped(GQ, group), grouped(HD, group), grouped(HD, group),
                grouped(GQ, group), grouped(GQ, group), grouped(8, group), shared(HD // 2),
                shared(HD // 2), shared(width),
            ] + [whole(x.shape) for x in joined],
            out_specs=(grouped(GD), *[whole(dims) for dims in grad_dims]),
            scratch_shapes=[pltpu.VMEM((HD, count), F32)] * 2 + [pltpu.VMEM((count, HD), BF16)] * 2,
            compiler_params=params,
            cost_estimate=cost(9),
            name="attend_back",
        )(
            after(ids, *sent), need, starts, q, k, v, d_att, att, lse, cos, sin, normed, *joined,
        )

    d_0, grads_a = attend_back(0, sent, [], [(4, quarter, GD)])
    sent = [run_1.step(d_0), run_2.step(d_0)]
    d_1, grads_b = attend_back(1, sent, [], [(4, quarter, GD)])
    sent = [run_1.step(d_1), run_2.step(d_1)]
    d_2, *pair = attend_back(2, sent, [grads_a, grads_b], [(quarter, KVH * GD)] * 4)
    sent = [run_1.step(d_2), run_2.step(d_2)]
    run_3 = Stages(reduce_steps(*pair[:3], after(pair[3], *sent), {1: 0}))
    sent.append(run_3.step())

    d_tok = pl.pallas_call(
        input_kernel,
        out_shape=shape((width, count), F32),
        in_specs=vmem(7),
        out_specs=pl.BlockSpec(memory_space=pltpu.VMEM),
        scratch_shapes=[pltpu.VMEM((width + 2 * kv, count), BF16)],
        compiler_params=params,
        cost_estimate=cost(7),
        name="input_grad",
    )(after(tok, *sent), d_mid, w_full, gains, d_0, d_1, d_2)

    sent = run_3.step(d_tok)
    run_1.step(after(d_tok, sent))
    run_2.step(after(d_tok, sent))
    sent = run_3.step()
    run_1.step(sent)
    run_2.step(sent)
    sent = run_3.step()
    run_1.step(sent)
    run_3.step()
    sent = run_3.step()
    while not (run_1.done() and run_2.done()):
        run_1.step(sent)
        run_2.step(sent)
    gain_shape = shape((rows,), F32)
    grad_gate, grad_up, grad_down, grad_out, grad_mlp_gain = pl.pallas_call(
        finish_hidden_kernel,
        out_shape=(
            shape((rows, hidden), F32), shape((rows, hidden), F32), shape((width, part), F32),
            shape((rows, width), F32), gain_shape,
        ),
        in_specs=[SMEM] + vmem(7),
        out_specs=vmem(5),
        compiler_params=most,
        cost_estimate=cost(5),
        name="finish_hidden",
    )(after(ids, sent), *run_1.now, *run_2.now, w_gate, w_up, gains)
    run_3.step(grad_mlp_gain)
    while not run_3.done():
        run_3.step()
    grad_query, grad_key, grad_value, grad_attn_gain = pl.pallas_call(
        finish_last_kernel,
        out_shape=(
            shape((rows, width), F32), shape((rows, kv), F32), shape((rows, kv), F32), gain_shape
        ),
        in_specs=[SMEM] + vmem(6),
        out_specs=vmem(4),
        compiler_params=most,
        cost_estimate=cost(3),
        name="finish_last",
    )(ids, *run_3.now, w_query, w_key, w_value, gains)
    grad_down = grad_down.T
    return (
        out.T, d_tok.T, grad_query, grad_key, grad_value, grad_out, grad_attn_gain,
        grad_gate, grad_up, grad_down, grad_mlp_gain,
    )


def solution(mesh):
    everywhere = P(("rep", "shard"), None)
    weight = P("shard", None)
    gain = P("shard")
    return jax.shard_map(
        functools.partial(shards, mesh.shape["rep"]),
        mesh=mesh,
        in_specs=(
            everywhere, everywhere, everywhere, weight, weight, weight, weight, gain, weight, weight,
            weight, gain,
        ),
        out_specs=(
            everywhere, everywhere, weight, weight, weight, weight, gain, weight, weight, weight, gain,
        ),
        check_vma=False,
    )
```
